512 devices in a mesh: rep: 32 (over x, y_hi, core), fsdp: 16 (over z, y_lo).
Axes of the slice: x: 4, y: 8 (y_hi: 4, y_lo: 2; y = y_hi * 2 + y_lo), z: 8, core: 2. Of those that a mesh axis runs over, the one named last changes fastest.
Arguments:
- states: bfloat16 [65536, 4096], P(('rep', 'fsdp'))
- norm_gain: float32 [4096], replicated, may hold values from 0.5 to 1.5
- key_cotangent: bfloat16 [65536, 512], P(('rep', 'fsdp')), may hold values from -0.125 to 0.125
- key_weight: bfloat16 [32, 4096, 512], P('rep', 'fsdp'), may hold values from -0.09375 to 0.09375
- center_params: float32 [256, 4096], P('fsdp'), may hold values from -6 to 6
- replica_params: float32 [32, 256, 4096], P('rep', 'fsdp'), may hold values from -6 to 6
- momentum: float32 [256, 4096], P('fsdp'), may hold values from -3 to 3
Outputs:
- keys: bfloat16 [65536, 512], P(('rep', 'fsdp'))
- state_grad: bfloat16 [65536, 4096], P(('rep', 'fsdp'))
- weight_grad: bfloat16 [32, 4096, 512], P('rep', 'fsdp')
- new_center: float32 [256, 4096], P('fsdp')
- new_momentum: float32 [256, 4096], P('fsdp')
The draws below stay inside these ranges and needn't reach their ends.
All inputs are finite; a program needn't handle non-finite values.
Results may differ from the reference program's by a relative error of at most 0.022.
Values may be sent and summed in bfloat16 or wider, within the bound.
A program may use at most 64 MiB of HBM per device.

```python
import math
import jax
import jax.numpy as jnp
from jax import lax

D = 4096
KW = 512
TOK_DEV = 128
TOKENS_REP = 2048
ROWS = 65536
REPLICAS = 32
FRAG_ROWS = 256
N_REP = 32
N_FSDP = 16


def draw_states(key, part):
    key = jax.random.fold_in(key, 11)
    first, second, third = jax.random.split(key, 3)
    row_scale = jnp.exp(jax.random.uniform(first, (ROWS, 1), jnp.float32) * math.log(10.0))
    col_scale = jnp.exp(jax.random.uniform(second, (1, D), jnp.float32) * math.log(10.0))
    base = jax.random.normal(third, (ROWS, D), jnp.float32)
    return (base * row_scale * col_scale * 0.25).astype(jnp.bfloat16)


def block_scale(own_key, extent, pieces, smallest, top_value):
    gain = 1.0
    for position, blocks in pieces:
        steps = jax.random.uniform(jax.random.fold_in(jax.random.fold_in(own_key, 6), position), (blocks,), jnp.float32, smallest / len(pieces), top_value / len(pieces))
        gain = gain * jnp.repeat(jnp.exp(steps), extent[position] // blocks).reshape((-1,) + (1,) * (len(extent) - 1 - position))
    return gain


def bell_draw(rng, shape, spread, most, cuts=(), held_as=jnp.bfloat16):
    level = block_scale(rng, shape, cuts, -0.22, 0.18) if cuts else 1.0
    result = jax.random.normal(rng, shape, jnp.float32) * spread * level
    return jnp.minimum(jnp.maximum(result, -most), most).astype(held_as)


def setup_inputs(seed: int = 0) -> dict:
    arg_keys = jax.random.split(jax.random.key(seed), 8)
    states = draw_states(jax.random.fold_in(arg_keys[7], 71), 0)
    norm_gain = jnp.clip(1.0 + 0.1 * jax.random.normal(arg_keys[1], (D,), jnp.float32), 0.5, 1.5)
    key_cotangent = bell_draw(arg_keys[2], (ROWS, KW), TOKENS_REP ** -0.5, 0.125, ((0, 512),))
    key_weight = bell_draw(arg_keys[3], (REPLICAS, D, KW), D ** -0.5, 0.09375, ((0, 32), (1, 16)))
    center_params = bell_draw(arg_keys[4], (FRAG_ROWS, D), 1.0, 6.0, ((0, 16),), jnp.float32)
    replica_params = bell_draw(arg_keys[5], (REPLICAS, FRAG_ROWS, D), 1.0, 6.0, ((0, 32), (1, 16)), jnp.float32)
    momentum = bell_draw(arg_keys[6], (FRAG_ROWS, D), 0.5, 3.0, ((0, 16),), jnp.float32)
    return {"states": states, "norm_gain": norm_gain, "key_cotangent": key_cotangent, "key_weight": key_weight, "center_params": center_params, "replica_params": replica_params, "momentum": momentum}


def replica_pass(items, norm_gain):
    rows, cotan, weight = items
    x = rows.astype(jnp.float32)
    inverse = lax.rsqrt(lax.optimization_barrier(jnp.mean(x * x, axis=-1, keepdims=True)) + 1e-05)
    scaled = x * inverse
    normed = (scaled * norm_gain).astype(jnp.bfloat16)
    keys = jnp.dot(normed, weight, preferred_element_type=jnp.float32).astype(jnp.bfloat16)
    blocks_a = normed.reshape(N_FSDP, TOK_DEV, D).astype(jnp.float32)
    blocks_b = cotan.reshape(N_FSDP, TOK_DEV, KW).astype(jnp.float32)
    partial_terms = jnp.einsum('btd,btk->bdk', blocks_a, blocks_b).astype(jnp.bfloat16)
    partial_terms = lax.optimization_barrier(partial_terms)
    grad = lax.optimization_barrier(jnp.sum(partial_terms.astype(jnp.float32), axis=0)).astype(jnp.bfloat16)
    upstream = lax.dot_general(cotan, weight, (((1,), (1,)), ((), ())), preferred_element_type=jnp.float32) * norm_gain
    mixed = lax.optimization_barrier(jnp.mean(upstream * scaled, axis=-1, keepdims=True))
    state_grad = (inverse * (upstream - scaled * mixed)).astype(jnp.bfloat16)
    return (keys, state_grad, grad)

def reference(states, norm_gain, key_cotangent, key_weight, center_params, replica_params, momentum):
    stacked = states.reshape(N_REP, TOKENS_REP, D)
    cotans = key_cotangent.reshape(N_REP, TOKENS_REP, KW)
    keys, state_grad, weight_grad = lax.map(lambda items: replica_pass(items, norm_gain), (stacked, cotans, key_weight))
    drift = lax.optimization_barrier(jnp.sum(center_params[None] - replica_params, axis=0)) / N_REP
    new_momentum = 0.9 * momentum + drift
    new_center = center_params - 0.7 * (drift + 0.9 * new_momentum)
    return (keys.reshape(ROWS, KW), state_grad.reshape(ROWS, D), weight_grad, new_center, new_momentum)
```

```python
import functools

import jax
import jax.numpy as jnp
from jax import lax
from jax.experimental import pallas as pl
from jax.experimental.pallas import tpu as pltpu
from jax.sharding import PartitionSpec as P

MESH = pl.DeviceIdType.MESH
F32, BF16 = jnp.float32, jnp.bfloat16

NX, NY, NC, NZ, NP = 4, 4, 2, 8, 2
PIECES = 4


def places():
    rep, fsdp = lax.axis_index("rep"), lax.axis_index("fsdp")
    here = dict(x=rep // (NY * NC), y=(rep // NC) % NY, c=rep % NC, z=fsdp // NP, p=fsdp % NP)

    def device(**other):
        at = {**here, **other}
        return ((at["x"] * NY + at["y"]) * NC + at["c"], at["z"] * NP + at["p"])

    return here, device


def step_kernel(
    states, gain, cot, weight, center, replica, momentum,
    keys_out, grad_out, wgrad_out, center_out, momentum_out,
    x_v, gain_v, cot_v, w_v, n_v, n_send, up_own, up_send, up_recv, partial, keys_acc, keys_send, keys_recv,
    sum_send, sum_recv,
    cen_v, rep_v, mom_v, rep_recv, half, x_recv, x_sum, y_recv, drift,
    loads, core_s, core_r, x_s, x_r, y_s, y_r, yg_s, yg_r, xg_s, xg_r, cg_s, cg_r,
    cot_s, cot_r, n_s, n_r, up_s, up_r, keys_s, keys_r, ag_s, ag_r, rs_s, rs_r,
):
    here, device = places()
    x, y, c, z, p = (here[k] for k in ("x", "y", "c", "z", "p"))
    tokens, width = cot.shape
    features = states.shape[1]
    share = weight.shape[1]
    rows = share // PIECES
    right, left = device(z=lax.rem(z + 1, NZ)), device(z=lax.rem(z + NZ - 1, NZ))
    pair, other_core = device(p=1 - p), device(c=1 - c)
    x_peer = [device(x=lax.rem(x + d, NX)) for d in range(1, NX)]
    y_peer = [device(y=lax.rem(y + d, NY)) for d in range(1, NY)]
    frag_rows, frag_cols = center.shape
    half_rows = frag_rows // NC
    x_cols = frag_cols // NX
    y_cols = x_cols // NY

    def remote(src, dst, send, recv, to):
        return pltpu.make_async_remote_copy(
            src_ref=src, dst_ref=dst, send_sem=send, recv_sem=recv, device_id=to, device_id_type=MESH
        )

    def column(cls, o):
        parity = p if cls == 0 else 1 - p
        return pl.multiple_of((lax.rem(z + o, NZ) * NP + parity) * share, share)

    local = [
        pltpu.make_async_copy(states, x_v, loads.at[0]),
        pltpu.make_async_copy(gain, gain_v, loads.at[1]),
        pltpu.make_async_copy(cot, cot_v.at[pl.ds(0, tokens)], loads.at[2]),
        pltpu.make_async_copy(weight.at[0], w_v.at[0], loads.at[3]),
        pltpu.make_async_copy(center, cen_v, loads.at[4]),
        pltpu.make_async_copy(replica.at[0], rep_v, loads.at[5]),
        pltpu.make_async_copy(momentum, mom_v, loads.at[6]),
    ]
    for copy in local:
        copy.start()

    barrier = pltpu.get_barrier_semaphore()
    peers = [right, left, pair, other_core] + x_peer + y_peer
    for peer in peers:
        pl.semaphore_signal(barrier, inc=1, device_id=peer, device_id_type=MESH)
    pl.semaphore_wait(barrier, len(peers))

    sends = []

    def send(*args):
        copy = remote(*args)
        copy.start()
        sends.append(copy)
        return copy

    def piece(i):
        return pl.ds(i * rows, rows)

    def slot(way, k):
        return (NZ - k) % NZ if way == 0 else k

    toward = (right, left)
    ring = [[{}, {}, {}, {}], [{}, {}, {}, {}]]
    count = [0, 0]

    def pass_on(way, k, i):
        src = weight.at[0, piece(i)] if k == 0 else w_v.at[slot(way, k), piece(i)]
        n = count[way]
        count[way] += 1
        ring[way][k][i] = send(
            src, w_v.at[slot(way, k + 1), piece(i)], ag_s.at[way, n], ag_r.at[way, n], toward[way]
        )

    for i in range(PIECES):
        for way in range(2):
            pass_on(way, 0, i)
    cot_copy = send(cot, cot_v.at[pl.ds(tokens, tokens)], cot_s, cot_r, pair)
    core_rows = pl.ds(pl.multiple_of(half_rows * (1 - c), half_rows), half_rows)
    core_copy = send(replica.at[0, core_rows], rep_recv, core_s, core_r, other_core)

    local[0].wait()
    local[1].wait()
    squares = jnp.zeros((tokens, share), F32)
    for b in range(features // share):
        block = x_v[:, pl.ds(b * share, share)].astype(F32)
        squares += block * block
    inverse = lax.rsqrt(jnp.sum(squares, axis=-1, keepdims=True) * (1.0 / features) + 1e-05)

    def normed(cls, o):
        at = pl.ds(column(cls, o), share)
        return (x_v[:, at].astype(F32) * inverse * gain_v[:, at]).astype(BF16)

    order = (4, 3, 5, 2, 6, 1, 7, 0)
    n_copy = {}
    for o in order:
        n_send[o] = normed(1, o)
        n_copy[o] = send(n_send.at[o], n_v.at[o, pl.ds(tokens, tokens)], n_s.at[o], n_r.at[o], pair)
    for o in order:
        n_v[o, pl.ds(0, tokens)] = normed(0, o)
    local[2].wait()
    local[3].wait()

    def upstream(o):
        up = lax.dot_general(cot_v[...], w_v[o], (((1,), (1,)), ((), ())), preferred_element_type=F32)
        up_own[o] = up[:tokens]
        up_send[o] = up[tokens:].astype(BF16)

    def outer_half():
        local[4].wait()
        local[5].wait()
        core_copy.wait_recv()
        mine = pl.ds(pl.multiple_of(half_rows * c, half_rows), half_rows)
        middle = cen_v[mine]
        half[...] = (middle - rep_v[mine]) + (middle - rep_recv[...])
        copies = []
        for d in range(1, NX):
            cols = pl.ds(pl.multiple_of(lax.rem(x + d, NX) * x_cols, x_cols), x_cols)
            copies.append(send(half.at[:, cols], x_recv.at[d - 1], x_s.at[d - 1], x_r.at[d - 1], x_peer[d - 1]))
        return copies

    def outer_x(copies):
        for copy in copies:
            copy.wait_recv()
        cols = pl.ds(pl.multiple_of(x * x_cols, x_cols), x_cols)
        x_sum[...] = half[:, cols] + x_recv[0] + x_recv[1] + x_recv[2]
        copies = []
        for d in range(1, NY):
            cols = pl.ds(pl.multiple_of(lax.rem(y + d, NY) * y_cols, y_cols), y_cols)
            copies.append(send(x_sum.at[:, cols], y_recv.at[d - 1], y_s.at[d - 1], y_r.at[d - 1], y_peer[d - 1]))
        return copies

    mine_rows = pl.ds(pl.multiple_of(half_rows * c, half_rows), half_rows)

    def outer_y(copies):
        for copy in copies:
            copy.wait_recv()
        cols = pl.ds(pl.multiple_of(y * y_cols, y_cols), y_cols)
        at = pl.ds(pl.multiple_of(x * x_cols + y * y_cols, y_cols), y_cols)
        drift[mine_rows, at] = x_sum[:, cols] + y_recv[0] + y_recv[1] + y_recv[2]
        part = drift.at[mine_rows, at]
        return [send(part, part, yg_s.at[d - 1], yg_r.at[d - 1], y_peer[d - 1]) for d in range(1, NY)]

    def outer_x_back(copies):
        for copy in copies:
            copy.wait_recv()
        part = drift.at[mine_rows, pl.ds(pl.multiple_of(x * x_cols, x_cols), x_cols)]
        return [send(part, part, xg_s.at[d - 1], xg_r.at[d - 1], x_peer[d - 1]) for d in range(1, NX)]

    def outer_core_back(copies):
        for copy in copies:
            copy.wait_recv()
        part = drift.at[mine_rows]
        return [send(part, part, cg_s, cg_r, other_core)]

    def outer_end(copies):
        for copy in copies:
            copy.wait_recv()
        local[6].wait()
        mean = drift[...] * (1.0 / (NX * NY * NC))
        moved = 0.9 * mom_v[...] + mean
        momentum_out[...] = moved
        center_out[...] = cen_v[...] - 0.7 * (mean + 0.9 * moved)

    def ring_step(k):
        for i in range(PIECES):
            for way in range(2):
                ring_piece(way, k, i)

    def ring_piece(way, k, i):
        if i in ring[way][k - 1]:
            ring[way][k - 1][i].wait_recv()
            if k < 3 or (k == 3 and i // (PIECES // 2) == way):
                pass_on(way, k, i)

    def weight_partial(o):
        n_copy[o].wait_recv()
        partial[o] = lax.dot_general(n_v[o], cot_v[...], (((0,), (0,)), ((), ())), preferred_element_type=F32)

    sums = [[{}, {}, {}, {}], [{}, {}, {}, {}]]
    sent = [0, 0]

    def target(way, s):
        return (4 - s) if way == 0 else (4 + s) % NZ

    def add_and_send(way, s, i):
        value = partial[target(way, s), piece(i)]
        if s and i in sums[way][s - 1]:
            sums[way][s - 1][i].wait_recv()
            value += sum_recv[way, s - 1, piece(i)].astype(F32)
        sum_send[way, s, piece(i)] = value.astype(BF16)
        n = sent[way]
        sent[way] += 1
        sums[way][s][i] = send(
            sum_send.at[way, s, piece(i)], sum_recv.at[way, s, piece(i)], rs_s.at[way, n], rs_r.at[way, n], toward[way]
        )

    first, second = range(PIECES // 2), range(PIECES // 2, PIECES)
    early = (list(first), list(second))
    late = (list(second), list(first))

    cot_copy.wait_recv()
    upstream(0)
    x_copies = outer_half()
    ring_step(1)
    for o in (7, 1):
        upstream(o)
    y_copies = outer_x(x_copies)
    ring_step(2)
    for o in (6, 2):
        upstream(o)
    yg_copies = outer_y(y_copies)
    weight_partial(4)
    for j in range(PIECES // 2):
        for way in range(2):
            add_and_send(way, 0, early[way][j])
    for o in (3, 5):
        weight_partial(o)
    ring_step(3)
    for j in range(PIECES // 2):
        for way in range(2):
            add_and_send(way, 1, late[way][j])
    for o in (5, 3):
        upstream(o)
    xg_copies = outer_x_back(yg_copies)
    for o in (2, 6):
        weight_partial(o)
    ring_step(4)
    upstream(4)

    for j in range(PIECES // 2):
        for way in range(2):
            add_and_send(way, 1, early[way][j])
    for o in (1, 7, 0):
        weight_partial(o)

    for o in range(NZ):
        product = jnp.dot(n_v[o], w_v[o], preferred_element_type=F32)
        if o == 0:
            keys_acc[...] = product
        else:
            keys_acc[...] += product
    keys_send[...] = keys_acc[pl.ds(tokens, tokens)].astype(BF16)
    keys_copy = send(keys_send, keys_recv, keys_s, keys_r, pair)
    up_copy = {}
    for o in order:
        up_copy[o] = send(up_send.at[o], up_recv.at[o], up_s.at[o], up_r.at[o], pair)

    def ring_sum(s, extra):
        for j in range(PIECES):
            for way in range(2):
                add_and_send(way, s, (late[way] + early[way])[j])
            extra[j]()

    state = {}

    def none():
        pass

    def keys_end():
        keys_copy.wait_recv()
        total = keys_acc[pl.ds(0, tokens)] + keys_recv[...].astype(F32)
        keys_out[...] = total.astype(BF16)
        state["mixed"] = jnp.sum(total * cot_v[pl.ds(0, tokens)].astype(F32), axis=-1, keepdims=True) * (1.0 / features)

    def state_grad(cls, o):
        at = pl.ds(column(cls, o), share)
        if cls == 0:
            up = up_own[o]
        else:
            up_copy[o].wait_recv()
            up = up_recv[o].astype(F32)
        scaled = x_v[:, at].astype(F32) * inverse
        grad_out[:, at] = (inverse * (up * gain_v[:, at] - scaled * state["mixed"])).astype(BF16)

    def core_back():
        state["cg"] = outer_core_back(xg_copies)

    def outer_last():
        outer_end(state["cg"])

    def grads(cls, offsets):
        def run():
            for o in offsets:
                state_grad(cls, o)
        return run

    ring_sum(2, (core_back, none, keys_end, grads(0, (0, 1, 2, 3))))
    ring_sum(3, (grads(0, (4, 5, 6, 7)), outer_last, grads(1, order[:2]), grads(1, order[2:4])))
    grads(1, order[4:])()
    for j in range(PIECES):
        for way in range(2):
            i = (late[way] + early[way])[j]
            sums[way][3][i].wait_recv()
            value = partial[0, piece(i)] + sum_recv[way, 3, piece(i)].astype(F32)
            if j < PIECES // 2:
                partial[0, piece(i)] = value
            else:
                wgrad_out[piece(i)] = value.astype(BF16)
    for copy in sends:
        copy.wait_send()


def store_kernel(*refs):
    n = len(refs) // 2
    sems = refs[-1]
    copies = [pltpu.make_async_copy(refs[i], refs[n + i], sems.at[i]) for i in range(n)]
    for copy in copies:
        copy.start()
    for copy in copies:
        copy.wait()


def on_device(states, norm_gain, key_cotangent, key_weight, center_params, replica_params, momentum):
    tokens, features = states.shape
    share, width = key_weight.shape[1:]
    frag_rows, frag_cols = center_params.shape
    half_rows, x_cols = frag_rows // NC, frag_cols // NX
    y_cols = x_cols // NY
    vmem, dma = pltpu.VMEM, pltpu.SemaphoreType.DMA
    pieces = 3 * PIECES + PIECES // 2
    results = [
        ((tokens, width), BF16),
        ((tokens, features), BF16),
        ((share, width), BF16),
        ((frag_rows, frag_cols), F32),
        ((frag_rows, frag_cols), F32),
    ]
    arguments = (
        states, norm_gain.reshape(1, features), key_cotangent, key_weight, center_params, replica_params, momentum
    )
    made = pl.pallas_call(
        step_kernel,
        out_shape=[pltpu.VMEM(shape, dtype) for shape, dtype in results],
        in_specs=[pl.BlockSpec(memory_space=pl.ANY)] * 7,
        out_specs=[pl.BlockSpec(memory_space=pltpu.VMEM)] * 5,
        scratch_shapes=[
            vmem((tokens, features), BF16),
            vmem((1, features), F32),
            vmem((2 * tokens, width), BF16),
            vmem((NZ, share, width), BF16),
            vmem((NZ, 2 * tokens, share), BF16),
            vmem((NZ, tokens, share), BF16),
            vmem((NZ, tokens, share), F32),
            vmem((NZ, tokens, share), BF16),
            vmem((NZ, tokens, share), BF16),
            vmem((NZ, share, width), F32),
            vmem((2 * tokens, width), F32),
            vmem((tokens, width), BF16),
            vmem((tokens, width), BF16),
            vmem((2, 4, share, width), BF16),
            vmem((2, 4, share, width), BF16),
            vmem((frag_rows, frag_cols), F32),
            vmem((frag_rows, frag_cols), F32),
            vmem((frag_rows, frag_cols), F32),
            vmem((half_rows, frag_cols), F32),
            vmem((half_rows, frag_cols), F32),
            vmem((NX - 1, half_rows, x_cols), F32),
            vmem((half_rows, x_cols), F32),
            vmem((NY - 1, half_rows, y_cols), F32),
            vmem((frag_rows, frag_cols), F32),
            dma((7,)),
            dma(()), dma(()),
            dma((NX - 1,)), dma((NX - 1,)),
            dma((NY - 1,)), dma((NY - 1,)),
            dma((NY - 1,)), dma((NY - 1,)),
            dma((NX - 1,)), dma((NX - 1,)),
            dma(()), dma(()),
            dma(()), dma(()),
            dma((NZ,)), dma((NZ,)),
            dma((NZ,)), dma((NZ,)),
            dma(()), dma(()),
            dma((2, pieces)), dma((2, pieces)),
            dma((2, pieces)), dma((2, pieces)),
        ],
        compiler_params=pltpu.CompilerParams(
            collective_id=0, has_side_effects=True, vmem_limit_bytes=36 * 2**20
        ),
        name="diloco_step",
    )(*(pltpu.with_memory_space_constraint(a, pltpu.HBM) for a in arguments))
    made = [pltpu.with_memory_space_constraint(a, pltpu.VMEM) for a in made]
    keys, state_grad, weight_grad, new_center, new_momentum = pl.pallas_call(
        store_kernel,
        out_shape=[jax.ShapeDtypeStruct(shape, dtype) for shape, dtype in results],
        in_specs=[pl.BlockSpec(memory_space=pltpu.VMEM)] * 5,
        out_specs=[pl.BlockSpec(memory_space=pl.ANY)] * 5,
        scratch_shapes=[dma((5,))],
        name="store",
    )(*made)
    return keys, state_grad, weight_grad.reshape(1, share, width), new_center, new_momentum


def solution(mesh):
    return jax.shard_map(
        on_device,
        mesh=mesh,
        in_specs=(
            P(("rep", "fsdp"), None),
            P(),
            P(("rep", "fsdp"), None),
            P("rep", "fsdp", None),
            P("fsdp", None),
            P("rep", "fsdp", None),
            P("fsdp", None),
        ),
        out_specs=(
            P(("rep", "fsdp"), None),
            P(("rep", "fsdp"), None),
            P("rep", "fsdp", None),
            P("fsdp", None),
            P("fsdp", None),
        ),
        check_vma=False,
    )
```

```python
import functools

import jax
import jax.numpy as jnp
from jax import lax
from jax.experimental import pallas as pl
from jax.experimental.pallas import tpu as pltpu
from jax.sharding import PartitionSpec as P

MESH = pl.DeviceIdType.MESH
F32, BF16 = jnp.float32, jnp.bfloat16

NX, NY, NC, NZ, NP = 4, 4, 2, 8, 2
PIECES = 4


def places():
    rep, fsdp = lax.axis_index("rep"), lax.axis_index("fsdp")
    here = dict(x=rep // (NY * NC), y=(rep // NC) % NY, c=rep % NC, z=fsdp // NP, p=fsdp % NP)

    def device(**other):
        at = {**here, **other}
        return ((at["x"] * NY + at["y"]) * NC + at["c"], at["z"] * NP + at["p"])

    return here, device


def step_kernel(
    states, gain, cot, weight, center, replica, momentum,
    keys_out, grad_out, wgrad_out, center_out, momentum_out,
    x_v, gain_v, cot_v, w_v, n_v, n_send, up_own, up_send, up_recv, partial, keys_acc, keys_send, keys_recv,
    sum_send, sum_recv,
    cen_v, rep_v, mom_v, rep_recv, half, x_recv, x_sum, y_recv, drift,
    loads, core_s, core_r, x_s, x_r, y_s, y_r, yg_s, yg_r, xg_s, xg_r, cg_s, cg_r,
    cot_s, cot_r, n_s, n_r, up_s, up_r, keys_s, keys_r, ag_s, ag_r, rs_s, rs_r, ready, whole,
):
    here, device = places()
    x, y, c, z, p = (here[k] for k in ("x", "y", "c", "z", "p"))
    tokens, width = cot.shape
    features = states.shape[1]
    share = weight.shape[1]
    rows = share // PIECES
    right, left = device(z=lax.rem(z + 1, NZ)), device(z=lax.rem(z + NZ - 1, NZ))
    pair, other_core = device(p=1 - p), device(c=1 - c)
    x_peer = [device(x=lax.rem(x + d, NX)) for d in range(1, NX)]
    y_peer = [device(y=lax.rem(y + d, NY)) for d in range(1, NY)]
    frag_rows, frag_cols = center.shape
    half_rows = frag_rows // NC
    x_cols = frag_cols // NX
    y_cols = x_cols // NY

    def remote(src, dst, send, recv, to):
        return pltpu.make_async_remote_copy(
            src_ref=src, dst_ref=dst, send_sem=send, recv_sem=recv, device_id=to, device_id_type=MESH
        )

    def column(cls, o):
        parity = p if cls == 0 else 1 - p
        return pl.multiple_of((lax.rem(z + o, NZ) * NP + parity) * share, share)

    local = [
        pltpu.make_async_copy(states, x_v, loads.at[0]),
        pltpu.make_async_copy(gain, gain_v, loads.at[1]),
        pltpu.make_async_copy(cot, cot_v.at[pl.ds(0, tokens)], loads.at[2]),
        pltpu.make_async_copy(weight.at[0], w_v.at[0], loads.at[3]),
        pltpu.make_async_copy(center, cen_v, loads.at[4]),
        pltpu.make_async_copy(replica.at[0], rep_v, loads.at[5]),
        pltpu.make_async_copy(momentum, mom_v, loads.at[6]),
    ]
    for copy in local:
        copy.start()

    barrier = pltpu.get_barrier_semaphore()
    for peer in (right, left):
        pl.semaphore_signal(barrier, inc=1, device_id=peer, device_id_type=MESH)

    def tell(sem, **at):
        pl.semaphore_signal(sem, inc=1, device_id=device(**at), device_id_type=MESH)

    half_y = y // 2
    second = p + half_y - 2 * p * half_y
    edges = (("x", 0, 1), ("x", 1, 2), ("x", 0, 3), ("y", 0, 1), ("y", 0, 3), ("y", 3, 2), ("c", 1, 0))
    group = {"x": 0, "y": 1, "c": 2}
    for axis, low, high in edges:
        pl.when(here[axis] == low)(functools.partial(tell, barrier, **{axis: high}))
    pl.when(second == 0)(functools.partial(tell, barrier, p=1 - p))
    pl.semaphore_wait(barrier, 2 + jnp.minimum(x, 1) + jnp.minimum(y, 1) + (1 - c) + second)
    for axis, low, high in edges:
        pl.when(here[axis] == high)(functools.partial(tell, ready.at[group[axis]], **{axis: low}))
    pl.when(second == 1)(functools.partial(tell, ready.at[3], p=1 - p))

    def meet_first():
        @pl.when(c == 1)
        def _():
            pl.semaphore_wait(ready.at[2], 1)

        for axis, inner in (("x", (0, 1)), ("y", (0, 3))):
            for one, other in (inner, inner[::-1]):
                @pl.when(here[axis] == one)
                def _():
                    pl.semaphore_wait(ready.at[group[axis]], 2 if one == 0 else 1)
                    tell(whole.at[group[axis]], **{axis: other})

    def meet_second():
        for axis, inner, outer in (("x", (0, 1), (3, 2)), ("y", (0, 3), (1, 2))):
            for one, end in zip(inner, outer):
                @pl.when(here[axis] == one)
                def _():
                    pl.semaphore_wait(whole.at[group[axis]], 1)
                    tell(whole.at[group[axis]], **{axis: end})

    def meet_last(axis):
        for end in ((2, 3) if axis == "x" else (1, 2)):
            @pl.when(here[axis] == end)
            def _():
                pl.semaphore_wait(whole.at[group[axis]], 1)

    sends = []

    def send(*args):
        copy = remote(*args)
        copy.start()
        sends.append(copy)
        return copy

    def piece(i):
        return pl.ds(i * rows, rows)

    def slot(way, k):
        return (NZ - k) % NZ if way == 0 else k

    toward = (right, left)
    ring = [[{}, {}, {}, {}], [{}, {}, {}, {}]]
    count = [0, 0]

    def pass_on(way, k, i):
        src = weight.at[0, piece(i)] if k == 0 else w_v.at[slot(way, k), piece(i)]
        n = count[way]
        count[way] += 1
        ring[way][k][i] = send(
            src, w_v.at[slot(way, k + 1), piece(i)], ag_s.at[way, n], ag_r.at[way, n], toward[way]
        )

    for i in range(PIECES):
        for way in range(2):
            pass_on(way, 0, i)

    local[0].wait()
    local[1].wait()
    squares = jnp.zeros((tokens, share), F32)
    for b in range(features // share):
        block = x_v[:, pl.ds(b * share, share)].astype(F32)
        squares += block * block
    inverse = lax.rsqrt(jnp.sum(squares, axis=-1, keepdims=True) * (1.0 / features) + 1e-05)

    def normed(cls, o):
        at = pl.ds(column(cls, o), share)
        return (x_v[:, at].astype(F32) * inverse * gain_v[:, at]).astype(BF16)

    order = (4, 3, 5, 2, 6, 1, 7, 0)
    n_copy = {}
    for o in order:
        n_send[o] = normed(1, o)

    @pl.when(second == 0)
    def _():
        pl.semaphore_wait(ready.at[3], 1)

    cot_copy = send(cot, cot_v.at[pl.ds(tokens, tokens)], cot_s, cot_r, pair)

    def send_normed(*offsets):
        for o in offsets:
            n_copy[o] = send(n_send.at[o], n_v.at[o, pl.ds(tokens, tokens)], n_s.at[o], n_r.at[o], pair)

    send_normed(4, 3)
    for o in order:
        n_v[o, pl.ds(0, tokens)] = normed(0, o)
    local[2].wait()
    local[3].wait()

    def upstream(o):
        up = lax.dot_general(cot_v[...], w_v[o], (((1,), (1,)), ((), ())), preferred_element_type=F32)
        up_own[o] = up[:tokens]
        up_send[o] = up[tokens:].astype(BF16)

    def outer_start():
        meet_first()
        theirs = pl.ds(pl.multiple_of(half_rows * (1 - c), half_rows), half_rows)
        return [send(replica.at[0, theirs], rep_recv, core_s, core_r, other_core)]

    def outer_half(copies):
        local[4].wait()
        local[5].wait()
        for copy in copies:
            copy.wait_recv()
        mine = pl.ds(pl.multiple_of(half_rows * c, half_rows), half_rows)
        middle = cen_v[mine]
        half[...] = (middle - rep_v[mine]) + (middle - rep_recv[...])
        meet_last("x")
        copies = []
        for d in range(1, NX):
            cols = pl.ds(pl.multiple_of(lax.rem(x + d, NX) * x_cols, x_cols), x_cols)
            copies.append(send(half.at[:, cols], x_recv.at[d - 1], x_s.at[d - 1], x_r.at[d - 1], x_peer[d - 1]))
        return copies

    def outer_x(copies):
        for copy in copies:
            copy.wait_recv()
        cols = pl.ds(pl.multiple_of(x * x_cols, x_cols), x_cols)
        x_sum[...] = half[:, cols] + x_recv[0] + x_recv[1] + x_recv[2]
        meet_last("y")
        copies = []
        for d in range(1, NY):
            cols = pl.ds(pl.multiple_of(lax.rem(y + d, NY) * y_cols, y_cols), y_cols)
            copies.append(send(x_sum.at[:, cols], y_recv.at[d - 1], y_s.at[d - 1], y_r.at[d - 1], y_peer[d - 1]))
        return copies

    mine_rows = pl.ds(pl.multiple_of(half_rows * c, half_rows), half_rows)

    def outer_y(copies):
        for copy in copies:
            copy.wait_recv()
        cols = pl.ds(pl.multiple_of(y * y_cols, y_cols), y_cols)
        at = pl.ds(pl.multiple_of(x * x_cols + y * y_cols, y_cols), y_cols)
        drift[mine_rows, at] = x_sum[:, cols] + y_recv[0] + y_recv[1] + y_recv[2]
        part = drift.at[mine_rows, at]
        return [send(part, part, yg_s.at[d - 1], yg_r.at[d - 1], y_peer[d - 1]) for d in range(1, NY)]

    def outer_x_back(copies):
        for copy in copies:
            copy.wait_recv()
        part = drift.at[mine_rows, pl.ds(pl.multiple_of(x * x_cols, x_cols), x_cols)]
        return [send(part, part, xg_s.at[d - 1], xg_r.at[d - 1], x_peer[d - 1]) for d in range(1, NX)]

    def outer_core_back(copies):
        for copy in copies:
            copy.wait_recv()
        part = drift.at[mine_rows]
        return [send(part, part, cg_s, cg_r, other_core)]

    def outer_end(copies):
        for copy in copies:
            copy.wait_recv()
        local[6].wait()
        mean = drift[...] * (1.0 / (NX * NY * NC))
        moved = 0.9 * mom_v[...] + mean
        momentum_out[...] = moved
        center_out[...] = cen_v[...] - 0.7 * (mean + 0.9 * moved)

    def ring_step(k, beside={}):
        for i in range(PIECES):
            for way in range(2):
                ring_piece(way, k, i)
            send_normed(*beside.get(i, ()))

    def ring_piece(way, k, i):
        if i in ring[way][k - 1]:
            ring[way][k - 1][i].wait_recv()
            if k < 3 or (k == 3 and i // (PIECES // 2) == way):
                pass_on(way, k, i)

    def weight_partial(o):
        n_copy[o].wait_recv()
        partial[o] = lax.dot_general(n_v[o], cot_v[...], (((0,), (0,)), ((), ())), preferred_element_type=F32)

    sums = [[{}, {}, {}, {}], [{}, {}, {}, {}]]
    sent = [0, 0]

    def target(way, s):
        return (4 - s) if way == 0 else (4 + s) % NZ

    def add_and_send(way, s, i):
        value = partial[target(way, s), piece(i)]
        if s and i in sums[way][s - 1]:
            sums[way][s - 1][i].wait_recv()
            value += sum_recv[way, s - 1, piece(i)].astype(F32)
        sum_send[way, s, piece(i)] = value.astype(BF16)
        n = sent[way]
        sent[way] += 1
        sums[way][s][i] = send(
            sum_send.at[way, s, piece(i)], sum_recv.at[way, s, piece(i)], rs_s.at[way, n], rs_r.at[way, n], toward[way]
        )

    first, second = range(PIECES // 2), range(PIECES // 2, PIECES)
    early = (list(first), list(second))
    late = (list(second), list(first))

    ring_step(1, {0: (5,), 1: (2,), 2: (6,), 3: (1,)})
    core_copies = outer_start()
    ring_step(2, {0: (7,), 1: (0,)})
    meet_second()
    cot_copy.wait_recv()
    weight_partial(4)
    for j in range(PIECES // 2):
        for way in range(2):
            add_and_send(way, 0, early[way][j])
    for o in (3, 5):
        weight_partial(o)
    for o in (0, 7, 1):
        upstream(o)
    x_copies = outer_half(core_copies)
    ring_step(3)
    for j in range(PIECES // 2):
        for way in range(2):
            add_and_send(way, 1, late[way][j])
    for o in (6, 2):
        upstream(o)
    for o in (2, 6):
        weight_partial(o)
    y_copies = outer_x(x_copies)
    up_copy = {}

    def send_upstream(*offsets):
        for o in offsets:
            up_copy[o] = send(up_send.at[o], up_recv.at[o], up_s.at[o], up_r.at[o], pair)

    send_upstream(0, 7, 1)
    ring_step(4)
    for o in (5, 3, 4):
        upstream(o)
    for j in range(PIECES // 2):
        for way in range(2):
            add_and_send(way, 1, early[way][j])
    for o in (1, 7, 0):
        weight_partial(o)
    yg_copies = outer_y(y_copies)

    for o in range(NZ):
        product = jnp.dot(n_v[o], w_v[o], preferred_element_type=F32)
        if o == 0:
            keys_acc[...] = product
        else:
            keys_acc[...] += product
    keys_send[...] = keys_acc[pl.ds(tokens, tokens)].astype(BF16)
    keys_copy = send(keys_send, keys_recv, keys_s, keys_r, pair)
    send_upstream(6, 2, 5, 3, 4)

    def ring_sum(s, extra):
        for j in range(PIECES):
            for way in range(2):
                add_and_send(way, s, (late[way] + early[way])[j])
            extra[j]()

    state = {}

    def none():
        pass

    def keys_end():
        keys_copy.wait_recv()
        total = keys_acc[pl.ds(0, tokens)] + keys_recv[...].astype(F32)
        keys_out[...] = total.astype(BF16)
        state["mixed"] = jnp.sum(total * cot_v[pl.ds(0, tokens)].astype(F32), axis=-1, keepdims=True) * (1.0 / features)

    def state_grad(cls, o):
        at = pl.ds(column(cls, o), share)
        if cls == 0:
            up = up_own[o]
        else:
            up_copy[o].wait_recv()
            up = up_recv[o].astype(F32)
        scaled = x_v[:, at].astype(F32) * inverse
        grad_out[:, at] = (inverse * (up * gain_v[:, at] - scaled * state["mixed"])).astype(BF16)

    def x_back():
        state["xg"] = outer_x_back(yg_copies)

    def core_back():
        state["cg"] = outer_core_back(state["xg"])

    def outer_last():
        outer_end(state["cg"])

    def grads(cls, offsets):
        def run():
            for o in offsets:
                state_grad(cls, o)
        return run

    def settle():
        for copy in sends[:-2 * PIECES]:
            copy.wait_send()

    ring_sum(2, (none, none, keys_end, none))
    ring_sum(3, (x_back, grads(0, order[:4]), grads(0, order[4:]), core_back))
    between = (grads(1, (0, 7, 1, 6)), grads(1, (2, 5, 3, 4)), outer_last, settle)
    for j in range(PIECES):
        between[j]()
        for way in range(2):
            i = (late[way] + early[way])[j]
            sums[way][3][i].wait_recv()
            value = partial[0, piece(i)] + sum_recv[way, 3, piece(i)].astype(F32)
            if j < PIECES // 2:
                partial[0, piece(i)] = value
            else:
                wgrad_out[piece(i)] = value.astype(BF16)
    for copy in sends[-2 * PIECES:]:
        copy.wait_send()


def store_kernel(*refs):
    n = len(refs) // 2
    sems = refs[-1]
    copies = [pltpu.make_async_copy(refs[i], refs[n + i], sems.at[i]) for i in range(n)]
    for copy in copies:
        copy.start()
    for copy in copies:
        copy.wait()


def on_device(states, norm_gain, key_cotangent, key_weight, center_params, replica_params, momentum):
    tokens, features = states.shape
    share, width = key_weight.shape[1:]
    frag_rows, frag_cols = center_params.shape
    half_rows, x_cols = frag_rows // NC, frag_cols // NX
    y_cols = x_cols // NY
    vmem, dma = pltpu.VMEM, pltpu.SemaphoreType.DMA
    pieces = 3 * PIECES + PIECES // 2
    results = [
        ((tokens, width), BF16),
        ((tokens, features), BF16),
        ((share, width), BF16),
        ((frag_rows, frag_cols), F32),
        ((frag_rows, frag_cols), F32),
    ]
    arguments = (
        states, norm_gain.reshape(1, features), key_cotangent, key_weight, center_params, replica_params, momentum
    )
    made = pl.pallas_call(
        step_kernel,
        out_shape=[pltpu.VMEM(shape, dtype) for shape, dtype in results],
        in_specs=[pl.BlockSpec(memory_space=pl.ANY)] * 7,
        out_specs=[pl.BlockSpec(memory_space=pltpu.VMEM)] * 5,
        scratch_shapes=[
            vmem((tokens, features), BF16),
            vmem((1, features), F32),
            vmem((2 * tokens, width), BF16),
            vmem((NZ, share, width), BF16),
            vmem((NZ, 2 * tokens, share), BF16),
            vmem((NZ, tokens, share), BF16),
            vmem((NZ, tokens, share), F32),
            vmem((NZ, tokens, share), BF16),
            vmem((NZ, tokens, share), BF16),
            vmem((NZ, share, width), F32),
            vmem((2 * tokens, width), F32),
            vmem((tokens, width), BF16),
            vmem((tokens, width), BF16),
            vmem((2, 4, share, width), BF16),
            vmem((2, 4, share, width), BF16),
            vmem((frag_rows, frag_cols), F32),
            vmem((frag_rows, frag_cols), F32),
            vmem((frag_rows, frag_cols), F32),
            vmem((half_rows, frag_cols), F32),
            vmem((half_rows, frag_cols), F32),
            vmem((NX - 1, half_rows, x_cols), F32),
            vmem((half_rows, x_cols), F32),
            vmem((NY - 1, half_rows, y_cols), F32),
            vmem((frag_rows, frag_cols), F32),
            dma((7,)),
            dma(()), dma(()),
            dma((NX - 1,)), dma((NX - 1,)),
            dma((NY - 1,)), dma((NY - 1,)),
            dma((NY - 1,)), dma((NY - 1,)),
            dma((NX - 1,)), dma((NX - 1,)),
            dma(()), dma(()),
            dma(()), dma(()),
            dma((NZ,)), dma((NZ,)),
            dma((NZ,)), dma((NZ,)),
            dma(()), dma(()),
            dma((2, pieces)), dma((2, pieces)),
            dma((2, pieces)), dma((2, pieces)),
            pltpu.SemaphoreType.REGULAR((4,)), pltpu.SemaphoreType.REGULAR((2,)),
        ],
        compiler_params=pltpu.CompilerParams(
            collective_id=0, has_side_effects=True, vmem_limit_bytes=36 * 2**20
        ),
        name="diloco_step",
    )(*(pltpu.with_memory_space_constraint(a, pltpu.HBM) for a in arguments))
    made = [pltpu.with_memory_space_constraint(a, pltpu.VMEM) for a in made]
    keys, state_grad, weight_grad, new_center, new_momentum = pl.pallas_call(
        store_kernel,
        out_shape=[jax.ShapeDtypeStruct(shape, dtype) for shape, dtype in results],
        in_specs=[pl.BlockSpec(memory_space=pltpu.VMEM)] * 5,
        out_specs=[pl.BlockSpec(memory_space=pl.ANY)] * 5,
        scratch_shapes=[dma((5,))],
        name="store",
    )(*made)
    return keys, state_grad, weight_grad.reshape(1, share, width), new_center, new_momentum


def solution(mesh):
    return jax.shard_map(
        on_device,
        mesh=mesh,
        in_specs=(
            P(("rep", "fsdp"), None),
            P(),
            P(("rep", "fsdp"), None),
            P("rep", "fsdp", None),
            P("fsdp", None),
            P("rep", "fsdp", None),
            P("fsdp", None),
        ),
        out_specs=(
            P(("rep", "fsdp"), None),
            P(("rep", "fsdp"), None),
            P("rep", "fsdp", None),
            P("fsdp", None),
            P("fsdp", None),
        ),
        check_vma=False,
    )
```

```python
import functools

import jax
import jax.numpy as jnp
from jax import lax
from jax.experimental import pallas as pl
from jax.experimental.pallas import tpu as pltpu
from jax.sharding import PartitionSpec as P

MESH = pl.DeviceIdType.MESH
F32, BF16 = jnp.float32, jnp.bfloat16

NX, NY, NC, NZ, NP = 4, 4, 2, 8, 2
PIECES = 4


def places():
    rep, fsdp = lax.axis_index("rep"), lax.axis_index("fsdp")
    here = dict(x=rep // (NY * NC), y=(rep // NC) % NY, c=rep % NC, z=fsdp // NP, p=fsdp % NP)

    def device(**other):
        at = {**here, **other}
        return ((at["x"] * NY + at["y"]) * NC + at["c"], at["z"] * NP + at["p"])

    return here, device


def step_kernel(
    states, gain, cot, weight, center, replica, momentum,
    keys_out, grad_out, wgrad_out, center_out, momentum_out,
    x_v, gain_v, cot_v, w_v, n_v, n_send, up_own, up_send, up_recv, partial, keys_acc, keys_send, keys_recv,
    sum_send, sum_recv,
    cen_v, rep_v, mom_v, rep_recv, half, x_recv, x_sum, y_recv, drift,
    loads, core_s, core_r, x_s, x_r, y_s, y_r, yg_s, yg_r, xg_s, xg_r, cg_s, cg_r,
    cot_s, cot_r, n_s, n_r, up_s, up_r, keys_s, keys_r, ag_s, ag_r, rs_s, rs_r, ready, whole,
):
    here, device = places()
    x, y, c, z, p = (here[k] for k in ("x", "y", "c", "z", "p"))
    tokens, width = cot.shape
    features = states.shape[1]
    share = weight.shape[1]
    rows = share // PIECES
    right, left = device(z=lax.rem(z + 1, NZ)), device(z=lax.rem(z + NZ - 1, NZ))
    pair, other_core = device(p=1 - p), device(c=1 - c)
    x_peer = [device(x=lax.rem(x + d, NX)) for d in range(1, NX)]
    y_peer = [device(y=lax.rem(y + d, NY)) for d in range(1, NY)]
    frag_rows, frag_cols = center.shape
    half_rows = frag_rows // NC
    x_cols = frag_cols // NX
    y_cols = x_cols // NY

    def remote(src, dst, send, recv, to):
        return pltpu.make_async_remote_copy(
            src_ref=src, dst_ref=dst, send_sem=send, recv_sem=recv, device_id=to, device_id_type=MESH
        )

    def column(cls, o):
        parity = p if cls == 0 else 1 - p
        return pl.multiple_of((lax.rem(z + o, NZ) * NP + parity) * share, share)

    local = [
        pltpu.make_async_copy(states, x_v, loads.at[0]),
        pltpu.make_async_copy(gain, gain_v, loads.at[1]),
        pltpu.make_async_copy(cot, cot_v.at[pl.ds(0, tokens)], loads.at[2]),
        pltpu.make_async_copy(weight.at[0], w_v.at[0], loads.at[3]),
        pltpu.make_async_copy(center, cen_v, loads.at[4]),
        pltpu.make_async_copy(replica.at[0], rep_v, loads.at[5]),
        pltpu.make_async_copy(momentum, mom_v, loads.at[6]),
    ]
    barrier = pltpu.get_barrier_semaphore()
    for peer in (right, left):
        pl.semaphore_signal(barrier, inc=1, device_id=peer, device_id_type=MESH)

    def tell(sem, **at):
        pl.semaphore_signal(sem, inc=1, device_id=device(**at), device_id_type=MESH)

    half_y = y // 2
    second = p + half_y - 2 * p * half_y
    edges = (("x", 0, 1), ("x", 1, 2), ("x", 0, 3), ("y", 0, 1), ("y", 0, 3), ("y", 3, 2), ("c", 1, 0))
    group = {"x": 0, "y": 1, "c": 2}
    for axis, low, high in edges:
        pl.when(here[axis] == low)(functools.partial(tell, barrier, **{axis: high}))
    pl.when(second == 0)(functools.partial(tell, barrier, p=1 - p))
    for copy in local:
        copy.start()
    pl.semaphore_wait(barrier, 2 + jnp.minimum(x, 1) + jnp.minimum(y, 1) + (1 - c) + second)
    for axis, low, high in edges:
        pl.when(here[axis] == high)(functools.partial(tell, ready.at[group[axis]], **{axis: low}))
    pl.when(second == 1)(functools.partial(tell, ready.at[3], p=1 - p))

    inner, outer = {"x": (0, 1), "y": (0, 3)}, {"x": (3, 2), "y": (1, 2)}

    def meet_first(axis):
        for one, other in (inner[axis], inner[axis][::-1]):
            @pl.when(here[axis] == one)
            def _():
                pl.semaphore_wait(ready.at[group[axis]], 2 if one == 0 else 1)
                tell(whole.at[group[axis]], **{axis: other})

    def meet_second(axis):
        for one, end in zip(inner[axis], outer[axis]):
            @pl.when(here[axis] == one)
            def _():
                pl.semaphore_wait(whole.at[group[axis]], 1)
                tell(whole.at[group[axis]], **{axis: end})

    def meet_last(axis):
        for end in outer[axis]:
            @pl.when(here[axis] == end)
            def _():
                pl.semaphore_wait(whole.at[group[axis]], 1)

    def send(*args):
        copy = remote(*args)
        copy.start()
        return copy

    def all_sent(like, sem):
        remote(like, like, sem, keys_r, pair).wait_send()

    def all_here(like, sem):
        remote(like, like, keys_s, sem, pair).wait_recv()

    def piece(i):
        return pl.ds(i * rows, rows)

    def slot(way, k):
        return (NZ - k) % NZ if way == 0 else k

    toward = (right, left)
    ring = [[{}, {}, {}, {}], [{}, {}, {}, {}]]
    count = [0, 0]

    def pass_on(way, k, i):
        src = weight.at[0, piece(i)] if k == 0 else w_v.at[slot(way, k), piece(i)]
        n = count[way]
        count[way] += 1
        ring[way][k][i] = send(
            src, w_v.at[slot(way, k + 1), piece(i)], ag_s, ag_r.at[way, n], toward[way]
        )

    for i in range(PIECES):
        for way in range(2):
            pass_on(way, 0, i)

    local[0].wait()
    local[1].wait()
    squares = jnp.zeros((tokens, share), F32)
    for b in range(features // share):
        block = x_v[:, pl.ds(b * share, share)].astype(F32)
        squares += block * block
    inverse = lax.rsqrt(jnp.sum(squares, axis=-1, keepdims=True) * (1.0 / features) + 1e-05)

    def normed(cls, o):
        at = pl.ds(column(cls, o), share)
        return (x_v[:, at].astype(F32) * inverse * gain_v[:, at]).astype(BF16)

    order = (4, 3, 5, 2, 6, 1, 7, 0)
    up_order = (0, 7, 1, 6, 2, 5, 3, 4)
    for o in order:
        n_send[order.index(o)] = normed(1, o)

    @pl.when(second == 0)
    def _():
        pl.semaphore_wait(ready.at[3], 1)

    cot_copy = send(cot, cot_v.at[pl.ds(tokens, tokens)], cot_s, cot_r, pair)

    def send_normed(*offsets):
        for o in offsets:
            n = order.index(o)
            send(n_send.at[n], n_v.at[o, pl.ds(tokens, tokens)], n_s, n_r.at[(n + 1) // 2 if n < 5 else 3], pair)

    send_normed(4, 3)
    for o in order:
        n_v[o, pl.ds(0, tokens)] = normed(0, o)
    local[2].wait()
    local[3].wait()

    def upstream(o):
        up = lax.dot_general(cot_v[...], w_v[o], (((1,), (1,)), ((), ())), preferred_element_type=F32)
        up_own[o] = up[:tokens]
        up_send[up_order.index(o)] = up[tokens:].astype(BF16)

    def outer_start():
        @pl.when(c == 1)
        def _():
            pl.semaphore_wait(ready.at[2], 1)

        theirs = pl.ds(pl.multiple_of(half_rows * (1 - c), half_rows), half_rows)
        state["core"] = send(replica.at[0, theirs], rep_recv, core_s, core_r, other_core)

    def outer_half():
        local[4].wait()
        local[5].wait()
        state["core"].wait_recv()
        mine = pl.ds(pl.multiple_of(half_rows * c, half_rows), half_rows)
        middle = cen_v[mine]
        half[...] = (middle - rep_v[mine]) + (middle - rep_recv[...])
        meet_last("x")
        for d in range(1, NX):
            cols = pl.ds(pl.multiple_of(lax.rem(x + d, NX) * x_cols, x_cols), x_cols)
            send(half.at[:, cols], x_recv.at[d - 1], x_s, x_r, x_peer[d - 1])

    def outer_x():
        all_here(x_recv, x_r)
        cols = pl.ds(pl.multiple_of(x * x_cols, x_cols), x_cols)
        x_sum[...] = half[:, cols] + x_recv[0] + x_recv[1] + x_recv[2]
        meet_last("y")
        for d in range(1, NY):
            cols = pl.ds(pl.multiple_of(lax.rem(y + d, NY) * y_cols, y_cols), y_cols)
            send(x_sum.at[:, cols], y_recv.at[d - 1], y_s, y_r, y_peer[d - 1])

    mine_rows = pl.ds(pl.multiple_of(half_rows * c, half_rows), half_rows)

    def outer_y():
        all_here(y_recv, y_r)
        cols = pl.ds(pl.multiple_of(y * y_cols, y_cols), y_cols)
        at = pl.ds(pl.multiple_of(x * x_cols + y * y_cols, y_cols), y_cols)
        drift[mine_rows, at] = x_sum[:, cols] + y_recv[0] + y_recv[1] + y_recv[2]
        part = drift.at[mine_rows, at]
        for d in range(1, NY):
            send(part, part, yg_s, yg_r, y_peer[d - 1])

    def outer_x_back():
        all_here(y_recv, yg_r)
        part = drift.at[mine_rows, pl.ds(pl.multiple_of(x * x_cols, x_cols), x_cols)]
        for d in range(1, NX):
            send(part, part, xg_s, xg_r, x_peer[d - 1])

    def outer_core_back():
        all_here(x_recv, xg_r)
        part = drift.at[mine_rows]
        state["back"] = send(part, part, cg_s, cg_r, other_core)

    def outer_end():
        state["back"].wait_recv()
        local[6].wait()
        mean = drift[...] * (1.0 / (NX * NY * NC))
        moved = 0.9 * mom_v[...] + mean
        momentum_out[...] = moved
        center_out[...] = cen_v[...] - 0.7 * (mean + 0.9 * moved)

    def ring_step(k, beside={}):
        for i in range(PIECES):
            for way in range(2):
                ring_piece(way, k, i)
            beside.get(i, lambda: None)()

    def ring_piece(way, k, i):
        if i in ring[way][k - 1]:
            ring[way][k - 1][i].wait_recv()
            if k < 3 or (k == 3 and i // (PIECES // 2) == way):
                pass_on(way, k, i)

    def normed_here(first, last):
        all_here(n_send.at[pl.ds(first, last - first)], n_r.at[(first + 1) // 2])

    def weight_partial(o):
        partial[o] = lax.dot_general(n_v[o], cot_v[...], (((0,), (0,)), ((), ())), preferred_element_type=F32)

    sums = [[{}, {}, {}, {}], [{}, {}, {}, {}]]
    sent = [0, 0]

    def target(way, s):
        return (4 - s) if way == 0 else (4 + s) % NZ

    def add_and_send(way, s, i):
        value = partial[target(way, s), piece(i)]
        if s and i in sums[way][s - 1]:
            sums[way][s - 1][i].wait_recv()
            value += sum_recv[way, s - 1, piece(i)].astype(F32)
        sum_send[way, s, piece(i)] = value.astype(BF16)
        n = sent[way]
        sent[way] += 1
        sums[way][s][i] = send(
            sum_send.at[way, s, piece(i)], sum_recv.at[way, s, piece(i)], rs_s, rs_r.at[way, n], toward[way]
        )

    first, second = range(PIECES // 2), range(PIECES // 2, PIECES)
    early = (list(first), list(second))
    late = (list(second), list(first))

    def send_upstream(*offsets):
        for o in offsets:
            n = up_order.index(o)
            send(up_send.at[n], up_recv.at[n], up_s, up_r.at[n // 4], pair)

    state = {}

    def early_x():
        send_normed(5)
        meet_first("x")

    def early_core():
        send_normed(2)
        outer_start()

    def whole_x():
        send_normed(6)
        meet_second("x")

    def start_x():
        send_normed(1)
        outer_half()
        meet_first("y")

    ring_step(1, {0: early_x, 1: early_core, 2: whole_x, 3: start_x})
    ring_step(2, {0: lambda: send_normed(7), 1: lambda: send_normed(0), 3: lambda: meet_second("y")})
    cot_copy.wait_recv()
    normed_here(0, 1)
    weight_partial(4)
    for j in range(PIECES // 2):
        for way in range(2):
            add_and_send(way, 0, early[way][j])
    outer_x()
    normed_here(1, 3)
    for o in (3, 5):
        weight_partial(o)
    for o in (0, 7, 1):
        upstream(o)
    ring_step(3)
    for j in range(PIECES // 2):
        for way in range(2):
            add_and_send(way, 1, late[way][j])
    send_upstream(0, 7, 1)
    for o in (6, 2):
        upstream(o)
    normed_here(3, 5)
    for o in (2, 6):
        weight_partial(o)
    ring_step(4)
    for o in (5, 3, 4):
        upstream(o)
    for j in range(PIECES // 2):
        for way in range(2):
            add_and_send(way, 1, early[way][j])
    normed_here(5, 8)
    for o in (1, 7, 0):
        weight_partial(o)
    outer_y()
    for o in range(NZ):
        product = jnp.dot(n_v[o], w_v[o], preferred_element_type=F32)
        if o == 0:
            keys_acc[...] = product
        else:
            keys_acc[...] += product
    keys_send[...] = keys_acc[pl.ds(tokens, tokens)].astype(BF16)
    keys_copy = send(keys_send, keys_recv, keys_s, keys_r, pair)
    send_upstream(6, 2)

    def ring_sum(s, extra):
        for j in range(PIECES):
            for way in range(2):
                add_and_send(way, s, (late[way] + early[way])[j])
            extra[j]()

    def none():
        pass

    def keys_end():
        keys_copy.wait_recv()
        total = keys_acc[pl.ds(0, tokens)] + keys_recv[...].astype(F32)
        keys_out[...] = total.astype(BF16)
        state["mixed"] = jnp.sum(total * cot_v[pl.ds(0, tokens)].astype(F32), axis=-1, keepdims=True) * (1.0 / features)

    def state_grad(cls, o):
        at = pl.ds(column(cls, o), share)
        if cls == 0:
            up = up_own[o]
        else:
            up = up_recv[up_order.index(o)].astype(F32)
        scaled = x_v[:, at].astype(F32) * inverse
        grad_out[:, at] = (inverse * (up * gain_v[:, at] - scaled * state["mixed"])).astype(BF16)

    def grads(cls, offsets):
        def run():
            if cls == 1:
                half_of = up_order.index(offsets[0]) // 4
                all_here(up_recv.at[pl.ds(4 * half_of, 4)], up_r.at[half_of])
            for o in offsets:
                state_grad(cls, o)
        return run

    def settle():
        all_sent(w_v.at[pl.ds(0, NZ - 1)], ag_s)
        all_sent(n_send, n_s)
        all_sent(up_send, up_s)
        all_sent(x_recv, x_s)
        all_sent(y_recv, y_s)
        all_sent(y_recv, yg_s)
        all_sent(x_recv, xg_s)
        for copy in (cot_copy, keys_copy, state["core"], state["back"]):
            copy.wait_send()

    def keys_and_grads():
        keys_end()
        grads(0, order[:4])()

    ring_sum(2, (lambda: send_upstream(5, 3), lambda: send_upstream(4), none, none))

    def core_and_grads():
        outer_core_back()
        grads(0, order[4:])()

    ring_sum(3, (outer_x_back, none, keys_and_grads, core_and_grads))
    between = (grads(1, (0, 7, 1, 6)), grads(1, (2, 5, 3, 4)), outer_end, settle)
    for j in range(PIECES):
        between[j]()
        for way in range(2):
            i = (late[way] + early[way])[j]
            sums[way][3][i].wait_recv()
            value = partial[0, piece(i)] + sum_recv[way, 3, piece(i)].astype(F32)
            if j < PIECES // 2:
                partial[0, piece(i)] = value
            else:
                wgrad_out[piece(i)] = value.astype(BF16)
    all_sent(w_v.at[pl.ds(0, NZ - 1)], rs_s)


def store_kernel(*refs):
    n = len(refs) // 2
    sems = refs[-1]
    copies = [pltpu.make_async_copy(refs[i], refs[n + i], sems.at[i]) for i in range(n)]
    for copy in copies:
        copy.start()
    for copy in copies:
        copy.wait()


def on_device(states, norm_gain, key_cotangent, key_weight, center_params, replica_params, momentum):
    tokens, features = states.shape
    share, width = key_weight.shape[1:]
    frag_rows, frag_cols = center_params.shape
    half_rows, x_cols = frag_rows // NC, frag_cols // NX
    y_cols = x_cols // NY
    vmem, dma = pltpu.VMEM, pltpu.SemaphoreType.DMA
    pieces = 3 * PIECES + PIECES // 2
    results = [
        ((tokens, width), BF16),
        ((tokens, features), BF16),
        ((share, width), BF16),
        ((frag_rows, frag_cols), F32),
        ((frag_rows, frag_cols), F32),
    ]
    arguments = (
        states, norm_gain.reshape(1, features), key_cotangent, key_weight, center_params, replica_params, momentum
    )
    made = pl.pallas_call(
        step_kernel,
        out_shape=[pltpu.VMEM(shape, dtype) for shape, dtype in results],
        in_specs=[pl.BlockSpec(memory_space=pl.ANY)] * 7,
        out_specs=[pl.BlockSpec(memory_space=pltpu.VMEM)] * 5,
        scratch_shapes=[
            vmem((tokens, features), BF16),
            vmem((1, features), F32),
            vmem((2 * tokens, width), BF16),
            vmem((NZ, share, width), BF16),
            vmem((NZ, 2 * tokens, share), BF16),
            vmem((NZ, tokens, share), BF16),
            vmem((NZ, tokens, share), F32),
            vmem((NZ, tokens, share), BF16),
            vmem((NZ, tokens, share), BF16),
            vmem((NZ, share, width), F32),
            vmem((2 * tokens, width), F32),
            vmem((tokens, width), BF16),
            vmem((tokens, width), BF16),
            vmem((2, 4, share, width), BF16),
            vmem((2, 4, share, width), BF16),
            vmem((frag_rows, frag_cols), F32),
            vmem((frag_rows, frag_cols), F32),
            vmem((frag_rows, frag_cols), F32),
            vmem((half_rows, frag_cols), F32),
            vmem((half_rows, frag_cols), F32),
            vmem((NX - 1, half_rows, x_cols), F32),
            vmem((half_rows, x_cols), F32),
            vmem((NY - 1, half_rows, y_cols), F32),
            vmem((frag_rows, frag_cols), F32),
            dma((7,)),
            *[dma(())] * 12,
            dma(()), dma(()), dma(()), dma((4,)), dma(()), dma((2,)), dma(()), dma(()),
            dma(()), dma((2, pieces)), dma(()), dma((2, pieces)),
            pltpu.SemaphoreType.REGULAR((4,)), pltpu.SemaphoreType.REGULAR((2,)),
        ],
        compiler_params=pltpu.CompilerParams(
            collective_id=0, has_side_effects=True, vmem_limit_bytes=36 * 2**20
        ),
        name="diloco_step",
    )(*(pltpu.with_memory_space_constraint(a, pltpu.HBM) for a in arguments))
    made = [pltpu.with_memory_space_constraint(a, pltpu.VMEM) for a in made]
    keys, state_grad, weight_grad, new_center, new_momentum = pl.pallas_call(
        store_kernel,
        out_shape=[jax.ShapeDtypeStruct(shape, dtype) for shape, dtype in results],
        in_specs=[pl.BlockSpec(memory_space=pltpu.VMEM)] * 5,
        out_specs=[pl.BlockSpec(memory_space=pl.ANY)] * 5,
        scratch_shapes=[dma((5,))],
        name="store",
    )(*made)
    return keys, state_grad, weight_grad.reshape(1, share, width), new_center, new_momentum


def solution(mesh):
    return jax.shard_map(
        on_device,
        mesh=mesh,
        in_specs=(
            P(("rep", "fsdp"), None),
            P(),
            P(("rep", "fsdp"), None),
            P("rep", "fsdp", None),
            P("fsdp", None),
            P("rep", "fsdp", None),
            P("fsdp", None),
        ),
        out_specs=(
            P(("rep", "fsdp"), None),
            P(("rep", "fsdp"), None),
            P("rep", "fsdp", None),
            P("fsdp", None),
            P("fsdp", None),
        ),
        check_vma=False,
    )
```

```python
import functools

import jax
import jax.numpy as jnp
from jax import lax
from jax.experimental import pallas as pl
from jax.experimental.pallas import tpu as pltpu
from jax.sharding import PartitionSpec as P

MESH = pl.DeviceIdType.MESH
F32, BF16 = jnp.float32, jnp.bfloat16

NX, NY, NC, NZ, NP = 4, 4, 2, 8, 2
PIECES = 4


def places():
    rep, fsdp = lax.axis_index("rep"), lax.axis_index("fsdp")
    here = dict(x=rep // (NY * NC), y=(rep // NC) % NY, c=rep % NC, z=fsdp // NP, p=fsdp % NP)

    def device(**other):
        at = {**here, **other}
        return ((at["x"] * NY + at["y"]) * NC + at["c"], at["z"] * NP + at["p"])

    return here, device


def step_kernel(
    states, gain, cot, weight, center, replica, momentum,
    keys_out, grad_out, wgrad_out, center_out, momentum_out,
    x_v, gain_v, cot_v, w_v, n_v, n_send, up_own, up_send, up_recv, partial, keys_acc, keys_send, keys_recv,
    sum_send, sum_recv,
    cen_v, rep_v, mom_v, rep_recv, half, x_recv, x_sum, y_recv, drift,
    loads, core_s, core_r, x_s, x_r, y_s, y_r, yg_s, yg_r, xg_s, xg_r, cg_s, cg_r,
    cot_s, cot_r, n_s, n_r, up_s, up_r, keys_s, keys_r, ag_s, ag_r, rs_s, rs_r, ready, whole,
):
    here, device = places()
    x, y, c, z, p = (here[k] for k in ("x", "y", "c", "z", "p"))
    tokens, width = cot.shape
    features = states.shape[1]
    share = weight.shape[1]
    rows = share // PIECES
    right, left = device(z=lax.rem(z + 1, NZ)), device(z=lax.rem(z + NZ - 1, NZ))
    pair, other_core = device(p=1 - p), device(c=1 - c)
    x_peer = [device(x=lax.rem(x + d, NX)) for d in range(1, NX)]
    y_peer = [device(y=lax.rem(y + d, NY)) for d in range(1, NY)]
    frag_rows, frag_cols = center.shape
    half_rows = frag_rows // NC
    x_cols = frag_cols // NX
    y_cols = x_cols // NY

    def remote(src, dst, send, recv, to):
        return pltpu.make_async_remote_copy(
            src_ref=src, dst_ref=dst, send_sem=send, recv_sem=recv, device_id=to, device_id_type=MESH
        )

    def column(cls, o):
        parity = p if cls == 0 else 1 - p
        return pl.multiple_of((lax.rem(z + o, NZ) * NP + parity) * share, share)

    local = [
        pltpu.make_async_copy(states, x_v, loads.at[0]),
        pltpu.make_async_copy(gain, gain_v, loads.at[1]),
        pltpu.make_async_copy(cot, cot_v.at[pl.ds(0, tokens)], loads.at[2]),
        pltpu.make_async_copy(weight.at[0], w_v.at[0], loads.at[3]),
        pltpu.make_async_copy(center, cen_v, loads.at[4]),
        pltpu.make_async_copy(replica.at[0], rep_v, loads.at[5]),
        pltpu.make_async_copy(momentum, mom_v, loads.at[6]),
    ]
    barrier = pltpu.get_barrier_semaphore()
    def tell(sem, **at):
        pl.semaphore_signal(sem, inc=1, device_id=device(**at), device_id_type=MESH)

    pl.semaphore_signal(barrier, inc=1, device_id=left, device_id_type=MESH)
    pl.when(z < NZ - 1)(functools.partial(tell, barrier, z=lax.rem(z + 1, NZ)))

    half_y = y // 2
    second = p + half_y - 2 * p * half_y
    edges = (("x", 0, 1), ("x", 1, 2), ("x", 0, 3), ("y", 0, 1), ("y", 0, 3), ("y", 3, 2), ("c", 1, 0))
    group = {"x": 0, "y": 1, "c": 2}
    for axis, low, high in edges:
        pl.when(here[axis] == low)(functools.partial(tell, barrier, **{axis: high}))
    pl.when(second == 0)(functools.partial(tell, barrier, p=1 - p))
    for copy in local:
        copy.start()
    pl.semaphore_wait(barrier, 1 + jnp.minimum(z, 1) + jnp.minimum(x, 1) + jnp.minimum(y, 1) + (1 - c) + second)
    pl.when(z == NZ - 1)(functools.partial(tell, ready.at[4], z=0))
    for axis, low, high in edges:
        pl.when(here[axis] == high)(functools.partial(tell, ready.at[group[axis]], **{axis: low}))
    pl.when(second == 1)(functools.partial(tell, ready.at[3], p=1 - p))

    inner, outer = {"x": (0, 1), "y": (0, 3)}, {"x": (3, 2), "y": (1, 2)}

    def meet_first(axis):
        for one, other in (inner[axis], inner[axis][::-1]):
            @pl.when(here[axis] == one)
            def _():
                pl.semaphore_wait(ready.at[group[axis]], 2 if one == 0 else 1)
                tell(whole.at[group[axis]], **{axis: other})

    def meet_second(axis):
        for one, end in zip(inner[axis], outer[axis]):
            @pl.when(here[axis] == one)
            def _():
                pl.semaphore_wait(whole.at[group[axis]], 1)
                tell(whole.at[group[axis]], **{axis: end})

    def meet_last(axis):
        for end in outer[axis]:
            @pl.when(here[axis] == end)
            def _():
                pl.semaphore_wait(whole.at[group[axis]], 1)

    def send(*args):
        copy = remote(*args)
        copy.start()
        return copy

    def all_sent(like, sem):
        remote(like, like, sem, keys_r, pair).wait_send()

    def all_here(like, sem):
        remote(like, like, keys_s, sem, pair).wait_recv()

    def piece(i):
        return pl.ds(i * rows, rows)

    def slot(way, k):
        return (NZ - k) % NZ if way == 0 else k

    toward = (right, left)
    ring = [[{}, {}, {}, {}], [{}, {}, {}, {}]]
    count = [0, 0]

    def pass_on(way, k, i, start=True):
        src = weight.at[0, piece(i)] if k == 0 else w_v.at[slot(way, k), piece(i)]
        n = min(count[way], 3 * PIECES)
        count[way] += 1
        copy = remote(src, w_v.at[slot(way, k + 1), piece(i)], ag_s, ag_r.at[way, n], toward[way])
        ring[way][k][i] = copy
        if start:
            copy.start()

    for i in range(PIECES):
        for way in range(2):
            pass_on(way, 0, i, way == 0)

    def start_left():
        for copy in ring[1][0].values():
            copy.start()

    pl.when(z > 0)(start_left)

    local[0].wait()
    local[1].wait()
    squares = jnp.zeros((tokens, share), F32)
    for b in range(features // share):
        block = x_v[:, pl.ds(b * share, share)].astype(F32)
        squares += block * block
    inverse = lax.rsqrt(jnp.sum(squares, axis=-1, keepdims=True) * (1.0 / features) + 1e-05)

    def normed(cls, o):
        at = pl.ds(column(cls, o), share)
        return (x_v[:, at].astype(F32) * inverse * gain_v[:, at]).astype(BF16)

    order = (4, 3, 5, 2, 6, 1, 7, 0)
    up_order = (0, 7, 1, 6, 2, 5, 3, 4)
    for o in order:
        n_send[order.index(o)] = normed(1, o)

    @pl.when(second == 0)
    def _():
        pl.semaphore_wait(ready.at[3], 1)

    cot_copy = send(cot, cot_v.at[pl.ds(tokens, tokens)], cot_s, cot_r, pair)

    def send_normed(*offsets):
        for o in offsets:
            n = order.index(o)
            send(n_send.at[n], n_v.at[o, pl.ds(tokens, tokens)], n_s, n_r.at[(n + 1) // 2 if n < 5 else 3], pair)

    send_normed(4, 3)
    for o in order:
        n_v[o, pl.ds(0, tokens)] = normed(0, o)

    @pl.when(z == 0)
    def _():
        pl.semaphore_wait(ready.at[4], 1)
        start_left()

    local[2].wait()
    local[3].wait()

    def upstream(o):
        up = lax.dot_general(cot_v[...], w_v[o], (((1,), (1,)), ((), ())), preferred_element_type=F32)
        up_own[o] = up[:tokens]
        up_send[up_order.index(o)] = up[tokens:].astype(BF16)

    def outer_start():
        @pl.when(c == 1)
        def _():
            pl.semaphore_wait(ready.at[2], 1)

        theirs = pl.ds(pl.multiple_of(half_rows * (1 - c), half_rows), half_rows)
        state["core"] = send(replica.at[0, theirs], rep_recv, core_s, core_r, other_core)

    def outer_half():
        local[4].wait()
        local[5].wait()
        state["core"].wait_recv()
        mine = pl.ds(pl.multiple_of(half_rows * c, half_rows), half_rows)
        middle = cen_v[mine]
        half[...] = (middle - rep_v[mine]) + (middle - rep_recv[...])
        meet_last("x")
        for d in range(1, NX):
            cols = pl.ds(pl.multiple_of(lax.rem(x + d, NX) * x_cols, x_cols), x_cols)
            send(half.at[:, cols], x_recv.at[d - 1], x_s, x_r, x_peer[d - 1])

    def outer_x():
        all_here(x_recv, x_r)
        cols = pl.ds(pl.multiple_of(x * x_cols, x_cols), x_cols)
        x_sum[...] = half[:, cols] + x_recv[0] + x_recv[1] + x_recv[2]
        meet_last("y")
        for d in range(1, NY):
            cols = pl.ds(pl.multiple_of(lax.rem(y + d, NY) * y_cols, y_cols), y_cols)
            send(x_sum.at[:, cols], y_recv.at[d - 1], y_s, y_r, y_peer[d - 1])

    mine_rows = pl.ds(pl.multiple_of(half_rows * c, half_rows), half_rows)

    def outer_y():
        all_here(y_recv, y_r)
        cols = pl.ds(pl.multiple_of(y * y_cols, y_cols), y_cols)
        at = pl.ds(pl.multiple_of(x * x_cols + y * y_cols, y_cols), y_cols)
        drift[mine_rows, at] = x_sum[:, cols] + y_recv[0] + y_recv[1] + y_recv[2]
        part = drift.at[mine_rows, at]
        for d in range(1, NY):
            send(part, part, yg_s, yg_r, y_peer[d - 1])

    def outer_x_back():
        all_here(y_recv, yg_r)
        part = drift.at[mine_rows, pl.ds(pl.multiple_of(x * x_cols, x_cols), x_cols)]
        for d in range(1, NX):
            send(part, part, xg_s, xg_r, x_peer[d - 1])

    def outer_core_back():
        all_here(x_recv, xg_r)
        part = drift.at[mine_rows]
        state["back"] = send(part, part, cg_s, cg_r, other_core)

    def outer_end():
        state["back"].wait_recv()
        local[6].wait()
        mean = drift[...] * (1.0 / (NX * NY * NC))
        moved = 0.9 * mom_v[...] + mean
        momentum_out[...] = moved
        center_out[...] = cen_v[...] - 0.7 * (mean + 0.9 * moved)

    def ring_step(k, beside={}):
        for i in range(PIECES):
            for way in range(2):
                ring_piece(way, k, i)
            beside.get(i, lambda: None)()

    def ring_piece(way, k, i):
        ring[way][k - 1][i].wait_recv()
        if k < 3 or i // (PIECES // 2) == way:
            pass_on(way, k, i)

    def ring_end():
        for way in range(2):
            like = w_v.at[4, pl.ds(way * (PIECES // 2) * rows, (PIECES // 2) * rows)]
            all_here(like, ag_r.at[way, 3 * PIECES])

    def normed_here(first, last):
        all_here(n_send.at[pl.ds(first, last - first)], n_r.at[(first + 1) // 2])

    def weight_partial(o):
        partial[o] = lax.dot_general(n_v[o], cot_v[...], (((0,), (0,)), ((), ())), preferred_element_type=F32)

    sums = [[{}, {}, {}, {}], [{}, {}, {}, {}]]
    sent = [0, 0]

    def target(way, s):
        return (4 - s) if way == 0 else (4 + s) % NZ

    def add_and_send(way, s, i):
        value = partial[target(way, s), piece(i)]
        if s and i in sums[way][s - 1]:
            sums[way][s - 1][i].wait_recv()
            value += sum_recv[way, s - 1, piece(i)].astype(F32)
        sum_send[way, s, piece(i)] = value.astype(BF16)
        n = sent[way]
        sent[way] += 1
        sums[way][s][i] = send(
            sum_send.at[way, s, piece(i)], sum_recv.at[way, s, piece(i)], rs_s, rs_r.at[way, n], toward[way]
        )

    first, second = range(PIECES // 2), range(PIECES // 2, PIECES)
    early = (list(first), list(second))
    late = (list(second), list(first))

    def send_upstream(*offsets):
        for o in offsets:
            n = up_order.index(o)
            send(up_send.at[n], up_recv.at[n], up_s, up_r.at[n // 4], pair)

    state = {}

    def early_x():
        send_normed(5)
        meet_first("x")

    def early_core():
        send_normed(2)
        outer_start()

    def whole_x():
        send_normed(6)
        meet_second("x")

    def start_x():
        send_normed(1)
        outer_half()
        meet_first("y")

    ring_step(1, {0: early_x, 1: early_core, 2: whole_x, 3: start_x})
    ring_step(2, {0: lambda: send_normed(7), 1: lambda: send_normed(0), 3: lambda: meet_second("y")})
    cot_copy.wait_recv()
    normed_here(0, 1)
    weight_partial(4)
    for j in range(PIECES // 2):
        for way in range(2):
            add_and_send(way, 0, early[way][j])
    outer_x()
    normed_here(1, 3)
    for o in (3, 5):
        weight_partial(o)
    for o in (0, 7, 1):
        upstream(o)
    ring_step(3)
    for j in range(PIECES // 2):
        for way in range(2):
            add_and_send(way, 1, late[way][j])
    send_upstream(0, 7, 1)
    for o in (6, 2):
        upstream(o)
    normed_here(3, 5)
    for o in (2, 6):
        weight_partial(o)
    for o in (5, 3):
        upstream(o)
    for j in range(PIECES // 2):
        for way in range(2):
            add_and_send(way, 1, early[way][j])
    normed_here(5, 8)
    for o in (1, 7, 0):
        weight_partial(o)
    outer_y()
    def key_part(o):
        product = jnp.dot(n_v[o], w_v[o], preferred_element_type=F32)
        if o == 0:
            keys_acc[...] = product
        else:
            keys_acc[...] += product

    for o in (0, 7, 1, 6, 2, 5, 3):
        key_part(o)
    send_upstream(6, 2)

    def keys_start():
        ring_end()
        key_part(4)
        keys_send[...] = keys_acc[pl.ds(tokens, tokens)].astype(BF16)
        state["keys"] = send(keys_send, keys_recv, keys_s, keys_r, pair)
        upstream(4)
        send_upstream(4)

    def ring_sum(s, extra):
        for j in range(PIECES):
            for way in range(2):
                add_and_send(way, s, (late[way] + early[way])[j])
            extra[j]()

    def none():
        pass

    def keys_end():
        state["keys"].wait_recv()
        total = keys_acc[pl.ds(0, tokens)] + keys_recv[...].astype(F32)
        keys_out[...] = total.astype(BF16)
        state["mixed"] = jnp.sum(total * cot_v[pl.ds(0, tokens)].astype(F32), axis=-1, keepdims=True) * (1.0 / features)

    def state_grad(cls, o):
        at = pl.ds(column(cls, o), share)
        if cls == 0:
            up = up_own[o]
        else:
            up = up_recv[up_order.index(o)].astype(F32)
        scaled = x_v[:, at].astype(F32) * inverse
        grad_out[:, at] = (inverse * (up * gain_v[:, at] - scaled * state["mixed"])).astype(BF16)

    def grads(cls, offsets):
        def run():
            if cls == 1:
                half_of = up_order.index(offsets[0]) // 4
                all_here(up_recv.at[pl.ds(4 * half_of, 4)], up_r.at[half_of])
            for o in offsets:
                state_grad(cls, o)
        return run

    def settle():
        all_sent(w_v.at[pl.ds(0, NZ - 1)], ag_s)
        all_sent(n_send, n_s)
        all_sent(up_send, up_s)
        all_sent(x_recv, x_s)
        all_sent(y_recv, y_s)
        all_sent(y_recv, yg_s)
        all_sent(x_recv, xg_s)
        for copy in (cot_copy, state["keys"], state["core"], state["back"]):
            copy.wait_send()

    def keys_and_grads():
        keys_end()
        grads(0, order[:4])()

    ring_sum(2, (lambda: send_upstream(5, 3), keys_start, none, none))

    def core_and_grads():
        outer_core_back()
        keys_and_grads()

    ring_sum(3, (outer_x_back, none, none, core_and_grads))
    def rest():
        grads(0, order[4:])()
        grads(1, (0, 7, 1, 6))()

    between = (rest, grads(1, (2, 5, 3, 4)), outer_end, settle)
    for j in range(PIECES):
        between[j]()
        for way in range(2):
            i = (late[way] + early[way])[j]
            sums[way][3][i].wait_recv()
            value = partial[0, piece(i)] + sum_recv[way, 3, piece(i)].astype(F32)
            if j < PIECES // 2:
                partial[0, piece(i)] = value
            else:
                wgrad_out[piece(i)] = value.astype(BF16)
    all_sent(w_v.at[pl.ds(0, NZ - 1)], rs_s)


def store_kernel(*refs):
    n = len(refs) // 2
    sems = refs[-1]
    copies = [pltpu.make_async_copy(refs[i], refs[n + i], sems.at[i]) for i in range(n)]
    for copy in copies:
        copy.start()
    for copy in copies:
        copy.wait()


def on_device(states, norm_gain, key_cotangent, key_weight, center_params, replica_params, momentum):
    tokens, features = states.shape
    share, width = key_weight.shape[1:]
    frag_rows, frag_cols = center_params.shape
    half_rows, x_cols = frag_rows // NC, frag_cols // NX
    y_cols = x_cols // NY
    vmem, dma = pltpu.VMEM, pltpu.SemaphoreType.DMA
    pieces = 3 * PIECES + PIECES // 2
    results = [
        ((tokens, width), BF16),
        ((tokens, features), BF16),
        ((share, width), BF16),
        ((frag_rows, frag_cols), F32),
        ((frag_rows, frag_cols), F32),
    ]
    arguments = (
        states, norm_gain.reshape(1, features), key_cotangent, key_weight, center_params, replica_params, momentum
    )
    made = pl.pallas_call(
        step_kernel,
        out_shape=[pltpu.VMEM(shape, dtype) for shape, dtype in results],
        in_specs=[pl.BlockSpec(memory_space=pl.ANY)] * 7,
        out_specs=[pl.BlockSpec(memory_space=pltpu.VMEM)] * 5,
        scratch_shapes=[
            vmem((tokens, features), BF16),
            vmem((1, features), F32),
            vmem((2 * tokens, width), BF16),
            vmem((NZ, share, width), BF16),
            vmem((NZ, 2 * tokens, share), BF16),
            vmem((NZ, tokens, share), BF16),
            vmem((NZ, tokens, share), F32),
            vmem((NZ, tokens, share), BF16),
            vmem((NZ, tokens, share), BF16),
            vmem((NZ, share, width), F32),
            vmem((2 * tokens, width), F32),
            vmem((tokens, width), BF16),
            vmem((tokens, width), BF16),
            vmem((2, 4, share, width), BF16),
            vmem((2, 4, share, width), BF16),
            vmem((frag_rows, frag_cols), F32),
            vmem((frag_rows, frag_cols), F32),
            vmem((frag_rows, frag_cols), F32),
            vmem((half_rows, frag_cols), F32),
            vmem((half_rows, frag_cols), F32),
            vmem((NX - 1, half_rows, x_cols), F32),
            vmem((half_rows, x_cols), F32),
            vmem((NY - 1, half_rows, y_cols), F32),
            vmem((frag_rows, frag_cols), F32),
            dma((7,)),
            *[dma(())] * 12,
            dma(()), dma(()), dma(()), dma((4,)), dma(()), dma((2,)), dma(()), dma(()),
            dma(()), dma((2, 3 * PIECES + 1)), dma(()), dma((2, pieces)),
            pltpu.SemaphoreType.REGULAR((5,)), pltpu.SemaphoreType.REGULAR((2,)),
        ],
        compiler_params=pltpu.CompilerParams(
            collective_id=0, has_side_effects=True, vmem_limit_bytes=36 * 2**20
        ),
        name="diloco_step",
    )(*(pltpu.with_memory_space_constraint(a, pltpu.HBM) for a in arguments))
    made = [pltpu.with_memory_space_constraint(a, pltpu.VMEM) for a in made]
    keys, state_grad, weight_grad, new_center, new_momentum = pl.pallas_call(
        store_kernel,
        out_shape=[jax.ShapeDtypeStruct(shape, dtype) for shape, dtype in results],
        in_specs=[pl.BlockSpec(memory_space=pltpu.VMEM)] * 5,
        out_specs=[pl.BlockSpec(memory_space=pl.ANY)] * 5,
        scratch_shapes=[dma((5,))],
        name="store",
    )(*made)
    return keys, state_grad, weight_grad.reshape(1, share, width), new_center, new_momentum


def solution(mesh):
    return jax.shard_map(
        on_device,
        mesh=mesh,
        in_specs=(
            P(("rep", "fsdp"), None),
            P(),
            P(("rep", "fsdp"), None),
            P("rep", "fsdp", None),
            P("fsdp", None),
            P("rep", "fsdp", None),
            P("fsdp", None),
        ),
        out_specs=(
            P(("rep", "fsdp"), None),
            P(("rep", "fsdp"), None),
            P("rep", "fsdp", None),
            P("fsdp", None),
            P("fsdp", None),
        ),
        check_vma=False,
    )
```

```python
import functools

import jax
import jax.numpy as jnp
from jax import lax
from jax.experimental import pallas as pl
from jax.experimental.pallas import tpu as pltpu
from jax.sharding import PartitionSpec as P

MESH = pl.DeviceIdType.MESH
F32, BF16 = jnp.float32, jnp.bfloat16

NX, NY, NC, NZ, NP = 4, 4, 2, 8, 2
PIECES = 4


def places():
    rep, fsdp = lax.axis_index("rep"), lax.axis_index("fsdp")
    here = dict(x=rep // (NY * NC), y=(rep // NC) % NY, c=rep % NC, z=fsdp // NP, p=fsdp % NP)

    def device(**other):
        at = {**here, **other}
        return ((at["x"] * NY + at["y"]) * NC + at["c"], at["z"] * NP + at["p"])

    return here, device


def step_kernel(
    states, gain, cot, weight, center, replica, momentum,
    keys_out, grad_out, wgrad_out, center_out, momentum_out,
    x_v, gain_v, cot_v, w_v, n_v, n_send, up_own, up_send, up_recv, partial, keys_acc, keys_send, keys_recv,
    sum_send, sum_recv,
    cen_v, rep_v, mom_v, rep_recv, half, x_recv, x_sum, y_recv, drift,
    loads, core_s, core_r, x_s, x_r, y_s, y_r, yg_s, yg_r, xg_s, xg_r, cg_s, cg_r,
    cot_s, cot_r, n_s, n_r, up_s, up_r, keys_s, keys_r, ag_s, ag_r, rs_s, rs_r, far_s, far_r, ready, whole,
):
    here, device = places()
    x, y, c, z, p = (here[k] for k in ("x", "y", "c", "z", "p"))
    tokens, width = cot.shape
    features = states.shape[1]
    share = weight.shape[1]
    rows = share // PIECES
    right, left = device(z=lax.rem(z + 1, NZ)), device(z=lax.rem(z + NZ - 1, NZ))
    pair, other_core = device(p=1 - p), device(c=1 - c)
    x_peer = [device(x=lax.rem(x + d, NX)) for d in range(1, NX)]
    y_peer = [device(y=lax.rem(y + d, NY)) for d in range(1, NY)]
    frag_rows, frag_cols = center.shape
    half_rows = frag_rows // NC
    x_cols = frag_cols // NX
    y_cols = x_cols // NY

    def remote(src, dst, send, recv, to):
        return pltpu.make_async_remote_copy(
            src_ref=src, dst_ref=dst, send_sem=send, recv_sem=recv, device_id=to, device_id_type=MESH
        )

    def column(cls, o):
        parity = p if cls == 0 else 1 - p
        return pl.multiple_of((lax.rem(z + o, NZ) * NP + parity) * share, share)

    local = [
        pltpu.make_async_copy(states, x_v, loads.at[0]),
        pltpu.make_async_copy(gain, gain_v, loads.at[1]),
        pltpu.make_async_copy(cot, cot_v.at[pl.ds(0, tokens)], loads.at[2]),
        pltpu.make_async_copy(weight.at[0], w_v.at[0], loads.at[3]),
        pltpu.make_async_copy(center, cen_v, loads.at[4]),
        pltpu.make_async_copy(replica.at[0], rep_v, loads.at[5]),
        pltpu.make_async_copy(momentum, mom_v, loads.at[6]),
    ]
    barrier = pltpu.get_barrier_semaphore()
    def tell(sem, **at):
        pl.semaphore_signal(sem, inc=1, device_id=device(**at), device_id_type=MESH)

    pl.semaphore_signal(barrier, inc=1, device_id=left, device_id_type=MESH)
    pl.when(z < NZ - 1)(functools.partial(tell, barrier, z=lax.rem(z + 1, NZ)))

    half_y = y // 2
    second = p + half_y - 2 * p * half_y
    edges = (("x", 0, 1), ("x", 1, 2), ("x", 0, 3), ("y", 0, 1), ("y", 0, 3), ("y", 3, 2), ("c", 1, 0))
    group = {"x": 0, "y": 1, "c": 2}
    for axis, low, high in edges:
        pl.when(here[axis] == low)(functools.partial(tell, barrier, **{axis: high}))
    pl.when(second == 0)(functools.partial(tell, barrier, p=1 - p))
    for copy in local:
        copy.start()
    pl.semaphore_wait(barrier, 1 + jnp.minimum(z, 1) + jnp.minimum(x, 1) + jnp.minimum(y, 1) + (1 - c) + second)
    pl.when(z == NZ - 1)(functools.partial(tell, ready.at[4], z=0))
    for axis, low, high in edges:
        pl.when(here[axis] == high)(functools.partial(tell, ready.at[group[axis]], **{axis: low}))
    pl.when(second == 1)(functools.partial(tell, ready.at[3], p=1 - p))

    inner, outer = {"x": (0, 1), "y": (0, 3)}, {"x": (3, 2), "y": (1, 2)}

    def meet_first(axis):
        for one, other in (inner[axis], inner[axis][::-1]):
            @pl.when(here[axis] == one)
            def _():
                pl.semaphore_wait(ready.at[group[axis]], 2 if one == 0 else 1)
                tell(whole.at[group[axis]], **{axis: other})

    def meet_second(axis):
        for one, end in zip(inner[axis], outer[axis]):
            @pl.when(here[axis] == one)
            def _():
                pl.semaphore_wait(whole.at[group[axis]], 1)
                tell(whole.at[group[axis]], **{axis: end})

    def meet_last(axis):
        for end in outer[axis]:
            @pl.when(here[axis] == end)
            def _():
                pl.semaphore_wait(whole.at[group[axis]], 1)

    def send(*args):
        copy = remote(*args)
        copy.start()
        return copy

    def all_sent(like, sem):
        remote(like, like, sem, keys_r, pair).wait_send()

    def all_here(like, sem):
        remote(like, like, keys_s, sem, pair).wait_recv()

    def piece(i):
        if isinstance(i, slice):
            return pl.ds(i.start * rows, (i.stop - i.start) * rows)
        return pl.ds(i * rows, rows)

    def slot(way, k):
        return (NZ - k) % NZ if way == 0 else k

    toward = (right, left)
    ring = [[{}, {}, {}, {}], [{}, {}, {}, {}]]
    count = [0, 0]

    def pass_on(way, k, i, start=True):
        src = weight.at[0, piece(i)] if k == 0 else w_v.at[slot(way, k), piece(i)]
        n = count[way]
        count[way] += 1
        copy = remote(src, w_v.at[slot(way, k + 1), piece(i)], ag_s, ag_r.at[way, n], toward[way])
        ring[way][k][i] = copy
        if start:
            copy.start()

    for i in range(PIECES):
        for way in range(2):
            pass_on(way, 0, i, way == 0)

    def start_left():
        for copy in ring[1][0].values():
            copy.start()

    pl.when(z > 0)(start_left)

    local[0].wait()
    local[1].wait()
    squares = jnp.zeros((tokens, share), F32)
    for b in range(features // share):
        block = x_v[:, pl.ds(b * share, share)].astype(F32)
        squares += block * block
    inverse = lax.rsqrt(jnp.sum(squares, axis=-1, keepdims=True) * (1.0 / features) + 1e-05)

    def normed(cls, o):
        at = pl.ds(column(cls, o), share)
        return (x_v[:, at].astype(F32) * inverse * gain_v[:, at]).astype(BF16)

    order = (4, 3, 5, 2, 6, 1, 7, 0)
    up_order = (0, 7, 1, 6, 2, 5, 3, 4)
    for o in order:
        n_send[order.index(o)] = normed(1, o)

    @pl.when(second == 0)
    def _():
        pl.semaphore_wait(ready.at[3], 1)

    cot_copy = send(cot, cot_v.at[pl.ds(tokens, tokens)], cot_s, cot_r, pair)

    def send_normed(*offsets):
        for o in offsets:
            n = order.index(o)
            send(n_send.at[n], n_v.at[o, pl.ds(tokens, tokens)], n_s, n_r.at[(n + 1) // 2 if n < 5 else 3], pair)

    send_normed(4, 3)
    for o in order:
        n_v[o, pl.ds(0, tokens)] = normed(0, o)

    @pl.when(z == 0)
    def _():
        pl.semaphore_wait(ready.at[4], 1)
        start_left()

    local[2].wait()
    local[3].wait()

    def upstream(o):
        up = lax.dot_general(cot_v[...], w_v[o], (((1,), (1,)), ((), ())), preferred_element_type=F32)
        up_own[o] = up[:tokens]
        up_send[up_order.index(o)] = up[tokens:].astype(BF16)

    def outer_start():
        @pl.when(c == 1)
        def _():
            pl.semaphore_wait(ready.at[2], 1)

        theirs = pl.ds(pl.multiple_of(half_rows * (1 - c), half_rows), half_rows)
        state["core"] = send(replica.at[0, theirs], rep_recv, core_s, core_r, other_core)

    def outer_half():
        local[4].wait()
        local[5].wait()
        state["core"].wait_recv()
        mine = pl.ds(pl.multiple_of(half_rows * c, half_rows), half_rows)
        middle = cen_v[mine]
        half[...] = (middle - rep_v[mine]) + (middle - rep_recv[...])
        meet_last("x")
        for d in range(1, NX):
            cols = pl.ds(pl.multiple_of(lax.rem(x + d, NX) * x_cols, x_cols), x_cols)
            send(half.at[:, cols], x_recv.at[d - 1], x_s, x_r, x_peer[d - 1])

    def outer_x():
        all_here(x_recv, x_r)
        cols = pl.ds(pl.multiple_of(x * x_cols, x_cols), x_cols)
        x_sum[...] = half[:, cols] + x_recv[0] + x_recv[1] + x_recv[2]
        meet_last("y")
        for d in range(1, NY):
            cols = pl.ds(pl.multiple_of(lax.rem(y + d, NY) * y_cols, y_cols), y_cols)
            send(x_sum.at[:, cols], y_recv.at[d - 1], y_s, y_r, y_peer[d - 1])

    mine_rows = pl.ds(pl.multiple_of(half_rows * c, half_rows), half_rows)

    def outer_y():
        all_here(y_recv, y_r)
        cols = pl.ds(pl.multiple_of(y * y_cols, y_cols), y_cols)
        at = pl.ds(pl.multiple_of(x * x_cols + y * y_cols, y_cols), y_cols)
        drift[mine_rows, at] = x_sum[:, cols] + y_recv[0] + y_recv[1] + y_recv[2]
        part = drift.at[mine_rows, at]
        for d in range(1, NY):
            send(part, part, yg_s, yg_r, y_peer[d - 1])

    def outer_x_back():
        all_here(y_recv, yg_r)
        part = drift.at[mine_rows, pl.ds(pl.multiple_of(x * x_cols, x_cols), x_cols)]
        for d in range(1, NX):
            send(part, part, xg_s, xg_r, x_peer[d - 1])

    def outer_core_back():
        all_here(x_recv, xg_r)
        part = drift.at[mine_rows]
        state["back"] = send(part, part, cg_s, cg_r, other_core)

    def outer_end():
        state["back"].wait()
        local[6].wait()
        mean = drift[...] * (1.0 / (NX * NY * NC))
        moved = 0.9 * mom_v[...] + mean
        momentum_out[...] = moved
        center_out[...] = cen_v[...] - 0.7 * (mean + 0.9 * moved)

    def ring_step(k, beside={}):
        for i in range(PIECES):
            for way in range(2):
                ring_piece(way, k, i)
            beside.get(i, lambda: None)()

    far = (piece(slice(0, PIECES // 2)), piece(slice(PIECES // 2, PIECES)))

    def far_copy(way, part, sem):
        at = far[part]
        return remote(w_v.at[slot(way, 3), at], w_v.at[4, at], far_s.at[sem], far_r.at[part], toward[way])

    far_copies = (far_copy(1, 1, 0), far_copy(0, 0, 1))

    def ring_piece(way, k, i):
        ring[way][k - 1][i].wait_recv()
        if k < 3:
            pass_on(way, k, i)
        elif way == 0 and i == PIECES // 2 - 1:
            far_copies[1].start()
        elif way == 1 and i == PIECES - 1:
            far_copies[0].start()

    def ring_end():
        for part in range(2):
            all_here(w_v.at[4, far[part]], far_r.at[part])

    def normed_here(first, last):
        all_here(n_send.at[pl.ds(first, last - first)], n_r.at[(first + 1) // 2])

    def weight_partial(o):
        partial[o] = lax.dot_general(n_v[o], cot_v[...], (((0,), (0,)), ((), ())), preferred_element_type=F32)

    sums = [[{}, {}, {}, {}], [{}, {}, {}, {}]]

    def target(way, s):
        return (4 - s) if way == 0 else (4 + s) % NZ

    def sum_copy(way, s, i, sem):
        copy = remote(
            sum_send.at[way, s, piece(i)], sum_recv.at[way, s, piece(i)], sem, ag_r.at[way, (s - 1) * PIECES + i] if s else rs_r.at[way, i], toward[way]
        )
        sums[way][s][i] = copy
        return copy

    def arrived(way, s, i):
        sums[way][s][i].wait_recv()
        partial[target(way, s + 1), piece(i)] += sum_recv[way, s, piece(i)].astype(F32)

    def add_and_send(way, s, i):
        if s > 1:
            sums[way][s - 1][i].wait_recv()
            value = partial[target(way, s), piece(i)] + sum_recv[way, s - 1, piece(i)].astype(F32)
        else:
            come = functools.partial(arrived, way, 0, i)
            if way == 0 and i in first:
                pl.when(jnp.logical_and(z > 0, z < NZ - 1))(come)
            elif way == 1 and i in first:
                pl.when(jnp.logical_or(z == NZ - 3, z == NZ - 2))(come)
            elif way == 1:
                come()
            value = partial[target(way, s), piece(i)]
        sum_send[way, s, piece(i)] = value.astype(BF16)
        sum_copy(way, s, i, rs_s).start()

    far_ways = ((0, 0, z < NZ - 2), (1, 0, z >= NZ - 2), (1, 1, z >= 0))

    def far_sums():
        for way, part, when in far_ways:
            half_pieces = (first, second)[part]
            copies = [sum_copy(way, 0, i, far_s.at[2 + way + part]) for i in half_pieces]

            def go(way=way, copies=copies, half_pieces=half_pieces):
                for copy, i in zip(copies, half_pieces):
                    sum_send[way, 0, piece(i)] = partial[4, piece(i)].astype(BF16)
                    copy.start()

            pl.when(when)(go)

    first, second = range(PIECES // 2), range(PIECES // 2, PIECES)
    early = (list(first), list(second))
    late = (list(second), list(first))

    def send_upstream(*offsets):
        for o in offsets:
            n = up_order.index(o)
            send(up_send.at[n], up_recv.at[n], up_s, up_r.at[n // 4], pair)

    state = {}

    def early_x():
        send_normed(5)
        meet_first("x")

    def early_core():
        send_normed(2)
        outer_start()

    def whole_x():
        send_normed(6)
        meet_second("x")

    def start_x():
        send_normed(1)
        outer_half()
        meet_first("y")

    ring_step(1, {0: early_x, 1: early_core, 2: whole_x, 3: start_x})
    ring_step(2, {0: lambda: send_normed(7), 1: lambda: send_normed(0), 3: lambda: meet_second("y")})
    cot_copy.wait_recv()
    normed_here(0, 1)
    weight_partial(4)
    far_sums()
    outer_x()
    normed_here(1, 3)
    for o in (3, 5):
        weight_partial(o)
    for o in (0, 7, 1):
        upstream(o)
    ring_step(3)
    for j in range(PIECES // 2):
        for way in range(2):
            add_and_send(way, 1, late[way][j])
    send_upstream(0, 7, 1)
    for o in (6, 2):
        upstream(o)
    normed_here(3, 5)
    for o in (2, 6):
        weight_partial(o)
    for o in (5, 3):
        upstream(o)
    for j in range(PIECES // 2):
        for way in range(2):
            add_and_send(way, 1, early[way][j])
    normed_here(5, 8)
    for o in (1, 7, 0):
        weight_partial(o)
    outer_y()
    def key_part(o):
        product = jnp.dot(n_v[o], w_v[o], preferred_element_type=F32)
        if o == 0:
            keys_acc[...] = product
        else:
            keys_acc[...] += product

    for o in (0, 7, 1, 6, 2, 5, 3):
        key_part(o)
    send_upstream(6, 2)

    def keys_start():
        ring_end()
        key_part(4)
        keys_send[...] = keys_acc[pl.ds(tokens, tokens)].astype(BF16)
        state["keys"] = send(keys_send, keys_recv, keys_s, keys_r, pair)
        upstream(4)
        send_upstream(4)

    def ring_sum(s, extra):
        for j in range(PIECES):
            for way in range(2):
                add_and_send(way, s, (late[way] + early[way])[j])
            extra[j]()

    def none():
        pass

    def keys_end():
        state["keys"].wait_recv()
        total = keys_acc[pl.ds(0, tokens)] + keys_recv[...].astype(F32)
        keys_out[...] = total.astype(BF16)
        state["mixed"] = jnp.sum(total * cot_v[pl.ds(0, tokens)].astype(F32), axis=-1, keepdims=True) * (1.0 / features)

    def state_grad(cls, o):
        at = pl.ds(column(cls, o), share)
        if cls == 0:
            up = up_own[o]
        else:
            up = up_recv[up_order.index(o)].astype(F32)
        scaled = x_v[:, at].astype(F32) * inverse
        grad_out[:, at] = (inverse * (up * gain_v[:, at] - scaled * state["mixed"])).astype(BF16)

    def grads(cls, offsets):
        def run():
            if cls == 1:
                half_of = up_order.index(offsets[0]) // 4
                all_here(up_recv.at[pl.ds(4 * half_of, 4)], up_r.at[half_of])
            for o in offsets:
                state_grad(cls, o)
        return run

    def settle():
        all_sent(w_v.at[pl.ds(0, NZ - 2)], ag_s)
        for n, when in [(0, None), (1, None)] + [(2 + n, way[2]) for n, way in enumerate(far_ways)]:
            done = functools.partial(all_sent, w_v.at[4, far[0]], far_s.at[n])
            done() if when is None else pl.when(when)(done)
        all_sent(n_send, n_s)
        all_sent(up_send, up_s)
        all_sent(x_recv, x_s)
        all_sent(y_recv, y_s)
        all_sent(y_recv, yg_s)
        all_sent(x_recv, xg_s)
        for copy in (cot_copy, state["keys"], state["core"]):
            copy.wait_send()

    def keys_and_grads():
        keys_end()
        grads(0, order[:4])()

    ring_sum(2, (lambda: send_upstream(5, 3), keys_start, none, none))

    def core_and_grads():
        outer_core_back()
        keys_and_grads()

    ring_sum(3, (outer_x_back, none, none, core_and_grads))
    def rest():
        grads(0, order[4:])()
        grads(1, (0, 7, 1, 6))()

    def rest_settle():
        grads(1, (2, 5, 3, 4))()
        settle()

    between = (rest, rest_settle, outer_end, none)
    for j in range(PIECES):
        between[j]()
        for way in range(2):
            i = (late[way] + early[way])[j]
            sums[way][3][i].wait_recv()
            value = partial[0, piece(i)] + sum_recv[way, 3, piece(i)].astype(F32)
            if j < PIECES // 2:
                partial[0, piece(i)] = value
            else:
                wgrad_out[piece(i)] = value.astype(BF16)
    all_sent(w_v.at[pl.ds(0, NZ - 2)], rs_s)


def store_kernel(*refs):
    n = len(refs) // 2
    sems = refs[-1]
    copies = [pltpu.make_async_copy(refs[i], refs[n + i], sems.at[i]) for i in range(n)]
    for copy in copies:
        copy.start()
    for copy in copies:
        copy.wait()


def on_device(states, norm_gain, key_cotangent, key_weight, center_params, replica_params, momentum):
    tokens, features = states.shape
    share, width = key_weight.shape[1:]
    frag_rows, frag_cols = center_params.shape
    half_rows, x_cols = frag_rows // NC, frag_cols // NX
    y_cols = x_cols // NY
    vmem, dma = pltpu.VMEM, pltpu.SemaphoreType.DMA
    results = [
        ((tokens, width), BF16),
        ((tokens, features), BF16),
        ((share, width), BF16),
        ((frag_rows, frag_cols), F32),
        ((frag_rows, frag_cols), F32),
    ]
    arguments = (
        states, norm_gain.reshape(1, features), key_cotangent, key_weight, center_params, replica_params, momentum
    )
    made = pl.pallas_call(
        step_kernel,
        out_shape=[pltpu.VMEM(shape, dtype) for shape, dtype in results],
        in_specs=[pl.BlockSpec(memory_space=pl.ANY)] * 7,
        out_specs=[pl.BlockSpec(memory_space=pltpu.VMEM)] * 5,
        scratch_shapes=[
            vmem((tokens, features), BF16),
            vmem((1, features), F32),
            vmem((2 * tokens, width), BF16),
            vmem((NZ, share, width), BF16),
            vmem((NZ, 2 * tokens, share), BF16),
            vmem((NZ, tokens, share), BF16),
            vmem((NZ, tokens, share), F32),
            vmem((NZ, tokens, share), BF16),
            vmem((NZ, tokens, share), BF16),
            vmem((NZ, share, width), F32),
            vmem((2 * tokens, width), F32),
            vmem((tokens, width), BF16),
            vmem((tokens, width), BF16),
            vmem((2, 4, share, width), BF16),
            vmem((2, 4, share, width), BF16),
            vmem((frag_rows, frag_cols), F32),
            vmem((frag_rows, frag_cols), F32),
            vmem((frag_rows, frag_cols), F32),
            vmem((half_rows, frag_cols), F32),
            vmem((half_rows, frag_cols), F32),
            vmem((NX - 1, half_rows, x_cols), F32),
            vmem((half_rows, x_cols), F32),
            vmem((NY - 1, half_rows, y_cols), F32),
            vmem((frag_rows, frag_cols), F32),
            dma((7,)),
            *[dma(())] * 12,
            dma(()), dma(()), dma(()), dma((4,)), dma(()), dma((2,)), dma(()), dma(()),
            dma(()), dma((2, 3 * PIECES)), dma(()), dma((2, PIECES)), dma((5,)), dma((2,)),
            pltpu.SemaphoreType.REGULAR((5,)), pltpu.SemaphoreType.REGULAR((2,)),
        ],
        compiler_params=pltpu.CompilerParams(
            collective_id=0, has_side_effects=True, vmem_limit_bytes=36 * 2**20
        ),
        name="diloco_step",
    )(*(pltpu.with_memory_space_constraint(a, pltpu.HBM) for a in arguments))
    made = [pltpu.with_memory_space_constraint(a, pltpu.VMEM) for a in made]
    keys, state_grad, weight_grad, new_center, new_momentum = pl.pallas_call(
        store_kernel,
        out_shape=[jax.ShapeDtypeStruct(shape, dtype) for shape, dtype in results],
        in_specs=[pl.BlockSpec(memory_space=pltpu.VMEM)] * 5,
        out_specs=[pl.BlockSpec(memory_space=pl.ANY)] * 5,
        scratch_shapes=[dma((5,))],
        name="store",
    )(*made)
    return keys, state_grad, weight_grad.reshape(1, share, width), new_center, new_momentum


def solution(mesh):
    return jax.shard_map(
        on_device,
        mesh=mesh,
        in_specs=(
            P(("rep", "fsdp"), None),
            P(),
            P(("rep", "fsdp"), None),
            P("rep", "fsdp", None),
            P("fsdp", None),
            P("rep", "fsdp", None),
            P("fsdp", None),
        ),
        out_specs=(
            P(("rep", "fsdp"), None),
            P(("rep", "fsdp"), None),
            P("rep", "fsdp", None),
            P("fsdp", None),
            P("fsdp", None),
        ),
        check_vma=False,
    )
```
